512 devices in a mesh: row: 16 (over x_lo, z), col: 32 (over y, x_hi, core).
Axes of the slice: x: 4 (x_hi: 2, x_lo: 2; x = x_hi * 2 + x_lo), y: 8, z: 8, core: 2. Of those that a mesh axis runs over, the one named last changes fastest.
Arguments:
- projections: float32 [49152, 128], P(('row', 'col')), may hold values from -40 to 40
- partner: int32 [49152], P(('row', 'col')), may hold values from 0 to 49151, as said below
Outputs:
- losses: float32 [49152], P(('row', 'col'))
- grad: float32 [49152, 128], P(('row', 'col'))
The draws below stay inside these ranges and needn't reach their ends.
Inputs may be any that keep to these rules, and one draw needn't show every extreme that they name: Each view's partner is another view of the same aligned block of 96 views, and the partner of a view's partner is the view itself.
All inputs are finite; a program needn't handle non-finite values.
Results may differ from the reference program's by a relative error of at most 0.0066.
Values may be sent and summed in bfloat16 or wider, within the bound.
A program may use at most 64 MiB of HBM per device.

```python
import math
import jax
import jax.numpy as jnp
from jax import lax

PROJ = 128
V_DEV = 96
VIEWS = 49152


def pairing(key):
    key = jax.random.fold_in(key, 5)
    blocks = VIEWS // V_DEV
    keys = jax.random.split(key, blocks)
    orders = jax.vmap(lambda single: jax.random.permutation(single, V_DEV))(keys).astype(jnp.int32)
    swapped = orders.reshape(blocks, V_DEV // 2, 2)[:, :, ::-1].reshape(blocks, V_DEV)
    local = jax.vmap(lambda order, other: jnp.zeros((V_DEV,), jnp.int32).at[order].set(other))(orders, swapped)
    offsets = (jnp.arange(blocks, dtype=jnp.int32) * V_DEV)[:, None]
    return (local + offsets).reshape(VIEWS).astype(jnp.int32)


def draw_partner(key, part):
    return pairing(key)


def cluster_labels(count):
    position = jnp.arange(count, dtype=jnp.int32)
    span = position // 63
    within = position % 63 + 1
    level = (within >= 2).astype(jnp.int32) + (within >= 4).astype(jnp.int32) + (within >= 8).astype(jnp.int32)
    level = level + (within >= 16).astype(jnp.int32) + (within >= 32).astype(jnp.int32)
    return (span * 6 + level).astype(jnp.int32)


def draw_projections(key, part):
    partner = pairing(key)
    key = jax.random.fold_in(key, 17)
    key_cluster, key_center, key_image, key_noise, key_scale, key_weight = jax.random.split(key, 6)
    index = jnp.arange(VIEWS, dtype=jnp.int32)
    pair_id = jnp.minimum(index, partner)
    follower = (index > partner).astype(jnp.int32)
    leaders = jnp.argsort(follower, stable=True)[:VIEWS // 2].astype(jnp.int32)
    shuffled = leaders[jax.random.permutation(key_cluster, VIEWS // 2)]
    group_of = jnp.zeros((VIEWS,), jnp.int32).at[shuffled].set(cluster_labels(VIEWS // 2))
    clusters = group_of[pair_id]
    centers = jax.random.normal(key_center, (VIEWS // 2, PROJ), jnp.float32)
    images = jax.random.normal(key_image, (VIEWS, PROJ), jnp.float32)
    noise = jax.random.normal(key_noise, (VIEWS, PROJ), jnp.float32)
    row_scale = jnp.exp(jax.random.uniform(key_scale, (VIEWS, 1), jnp.float32, jnp.log(0.5), jnp.log(4.0)))
    center_weight = jax.random.uniform(key_weight, (VIEWS, 1), jnp.float32, 0.4, 1.1)
    value = row_scale * (center_weight * centers[clusters] + 0.25 * images[pair_id] + 0.25 * noise)
    return jnp.clip(value, -40.0, 40.0)


def setup_inputs(seed: int = 0) -> dict:
    arg_keys = jax.random.split(jax.random.key(seed), 3)
    return {
        "projections": draw_projections(jax.random.fold_in(arg_keys[2], 71), 0),
        "partner": draw_partner(jax.random.fold_in(arg_keys[2], 71), 0),
    }


inv_temp = 10.0
epsilon = 1e-06

def reference(projections, partner):
    scale = lax.rsqrt(lax.optimization_barrier(jnp.sum(projections * projections, axis=1, keepdims=True)) + epsilon)
    unit = (projections * scale).astype(jnp.bfloat16)
    unit_wide = unit.astype(jnp.float32)
    partner_unit = unit_wide[partner]
    positive = lax.optimization_barrier(jnp.sum(unit_wide * partner_unit, axis=1)) * inv_temp
    width = unit.shape[1]
    count = VIEWS // math.gcd(VIEWS, 512)
    view_ids = jnp.arange(VIEWS, dtype=jnp.int32)
    blocked_unit = unit_wide.reshape(count, -1, width)
    blocked_ids = view_ids.reshape(count, -1)

    def exp_scores(block_unit, block_ids):
        scores = jnp.einsum('rp,cp->rc', block_unit, unit_wide, precision=lax.Precision.HIGHEST) * inv_temp
        return jnp.where(block_ids[:, None] == view_ids[None, :], 0.0, jnp.exp(scores - inv_temp))

    def block_sums(packed):
        return lax.optimization_barrier(jnp.sum(exp_scores(packed[0], packed[1]), axis=1))
    totals = lax.map(block_sums, (blocked_unit, blocked_ids)).reshape(-1)

    def block_terms(carry, packed):
        block_unit, block_ids, block_totals = packed
        weights = (exp_scores(block_unit, block_ids) / block_totals[:, None]).astype(jnp.bfloat16).astype(jnp.float32)
        row_out = jnp.einsum('rc,cp->rp', weights, unit_wide, precision=lax.Precision.HIGHEST)
        carry = carry + jnp.einsum('rc,rp->cp', weights, block_unit, precision=lax.Precision.HIGHEST)
        return (carry, row_out)
    start = jnp.zeros((VIEWS, width), jnp.float32)
    col_part, row_part = lax.scan(block_terms, start, (blocked_unit, blocked_ids, totals.reshape(count, -1)))
    row_part = row_part.reshape(VIEWS, width)
    losses = inv_temp + jnp.log(totals) - positive
    dunit = inv_temp * (row_part + col_part - 2.0 * partner_unit)
    inner = lax.optimization_barrier(jnp.sum(projections * dunit, axis=1, keepdims=True))
    grad = scale * dunit - scale * scale * scale * projections * inner
    return (losses, grad)
```

```python
import functools

import jax
import jax.numpy as jnp
from jax import lax
from jax.experimental import pallas as pl
from jax.experimental.pallas import tpu as pltpu
from jax.sharding import PartitionSpec as P

inv_temp = 10.0
epsilon = 1e-06
log2e = 1.4426950408889634

V = 96
W = 128
NX, NY, NZ, NC = 4, 8, 8, 2
NR = NX * NY * NC
GROUP = NX * V
BLOCK = NC * GROUP
COLS = NR * V
ROWS = NZ * V
TILE = 128
ORDER = (0, 1, 7, 2, 6, 3, 5, 4)
FAR = (4, 3, 5, 2, 6, 1, 7)

MESH = pl.DeviceIdType.MESH


def kernel(
    proj_hbm, partner_hbm, losses_ref, grad_ref,
    proj_ref, partner_ref, ur, cu, probs, acc, rhs, invc, tps, tp, tr, tc, sbuf, rbuf,
    in_sem, x_send, x_recv, y_send, y_recv, k_send, k_recv, z_send, z_recv,
    tp_send, tp_recv, tr_send, tr_recv, tc_send, tc_recv, o_send, o_recv,
):
    proj_copy = pltpu.make_async_copy(proj_hbm, proj_ref, in_sem.at[0])
    partner_copy = pltpu.make_async_copy(partner_hbm, partner_ref, in_sem.at[1])
    proj_copy.start()
    partner_copy.start()

    row, col = lax.axis_index("row"), lax.axis_index("col")
    z, x_lo = row % NZ, row // NZ
    core, x_hi, y = col % NC, (col // NC) % 2, col // (2 * NC)
    x = x_hi * 2 + x_lo
    at_x = [(x + dx) % NX for dx in range(NX)]
    x_row = [(px % 2) * NZ for px in at_x]
    x_col = [(px // 2) * NC for px in at_x]
    y_col = [((y + dy) % NY) * (2 * NC) for dy in range(NY)]
    at_z = [(z + dz) % NZ for dz in range(NZ)]
    cores = (core, 1 - core)

    def device(dx, dy, dz, dk):
        return (x_row[dx % NX] + at_z[dz % NZ], y_col[dy % NY] + x_col[dx % NX] + cores[dk])

    started = []

    def remote(src, dst, send_sem, recv_sem, to):
        return pltpu.make_async_remote_copy(
            src_ref=src, dst_ref=dst, send_sem=send_sem, recv_sem=recv_sem,
            device_id=to, device_id_type=MESH,
        )

    def send(*args):
        copy = remote(*args)
        copy.start()
        started.append(copy)
        return copy

    barrier = pltpu.get_barrier_semaphore()
    peers = [device(dx, 0, 0, 0) for dx in range(1, NX)]
    peers += [device(0, dy, 0, 0) for dy in range(1, NY)]
    peers += [device(0, 0, dz, 0) for dz in range(1, NZ)]
    peers += [device(0, 0, 0, 1)]
    for peer in peers:
        pl.semaphore_signal(barrier, inc=1, device_id=peer, device_id_type=MESH)

    tps[...] = jnp.ones_like(tps)
    proj_copy.wait()
    proj = proj_ref[...]
    scale = lax.rsqrt(jnp.sum(proj * proj, axis=1, keepdims=True) + epsilon)
    unit = (proj * scale).astype(jnp.bfloat16)
    ur[pl.ds(0, V), :] = unit
    cu[pl.ds(0, V), :] = unit

    pl.semaphore_wait(barrier, len(peers))

    def block(rank, dx):
        return ur.at[pl.ds(rank * BLOCK + dx * V, V)]

    def pass_on(rank, dx):
        return send(block(rank, 0), block(rank, dx), x_send.at[rank, dx], x_recv.at[rank, dx],
                    device(-dx, 0, 0, 0))

    for dx in (1, 3, 2):
        pass_on(0, dx)
    y_copies = [
        send(block(0, 0), block(rank, 0), y_send.at[rank], y_recv.at[rank],
             device(0, -ORDER[rank], 0, 0))
        for rank in range(1, NY)
    ]
    z_copies = [
        send(cu.at[pl.ds(0, V)], cu.at[pl.ds(dz * V, V)], z_send.at[dz], z_recv.at[dz],
             device(0, 0, -dz, 0))
        for dz in FAR
    ]
    for rank in range(1, NY):
        y_copies[rank - 1].wait_recv()
        for dx in (1, 3, 2):
            pass_on(rank, dx)

    def share(rank):
        first = rank * BLOCK
        return remote(ur.at[pl.ds(first, GROUP)], ur.at[pl.ds(first + GROUP, GROUP)],
                      k_send.at[rank], k_recv.at[rank], device(0, 0, 0, 1))

    def share_when_whole(rank):
        for dx in (1, 3, 2):
            remote(block(rank, 0), block(rank, dx), x_send.at[rank, dx], x_recv.at[rank, dx],
                   device(-dx, 0, 0, 0)).wait_recv()
        share(rank).start()

    def scores(rank, diagonal):
        first = pl.multiple_of(rank * BLOCK, BLOCK)
        units = ur[pl.ds(first, BLOCK), :]
        for at in range(0, ROWS, TILE):
            dots = lax.dot_general(
                cu[pl.ds(at, TILE), :], units, (((1,), (1,)), ((), ())),
                preferred_element_type=jnp.float32,
            )
            values = jnp.exp2(dots * (inv_temp * log2e))
            if diagonal and at == 0:
                views = lax.broadcasted_iota(jnp.int32, (TILE, BLOCK), 0)
                others = lax.broadcasted_iota(jnp.int32, (TILE, BLOCK), 1)
                values = jnp.where((views == others) & (views < V), 0.0, values)
            total = values[:, :W]
            for lane in range(W, BLOCK, W):
                total = total + values[:, lane:lane + W]
            if diagonal:
                acc[pl.ds(at, TILE), :] = total
            else:
                acc[pl.ds(at, TILE), :] += total
            probs[pl.ds(at, TILE), pl.ds(first, BLOCK)] = values.astype(jnp.bfloat16)

    share_when_whole(0)
    for copy in z_copies:
        copy.wait_recv()
    share_when_whole(1)
    share(0).wait_recv()
    scores(0, True)

    def step(rank, carry):
        @pl.when(rank < NY - 1)
        def _():
            share_when_whole(rank + 1)

        share(rank).wait_recv()
        scores(rank, False)
        return carry

    lax.fori_loop(1, NY, step, 0)

    ones = jnp.ones((8, W), jnp.float32)
    for dz in range(NZ):
        sums = lax.dot_general(
            ones, acc[pl.ds(dz * V, V), :], (((1,), (1,)), ((), ())),
            precision=lax.Precision.HIGHEST, preferred_element_type=jnp.float32,
        )
        tps[dz, :, pl.ds(0, V)] = sums[:1]
    tp[pl.ds(0, 1)] = tps[pl.ds(0, 1)]
    p_totals = [
        send(tps.at[pl.ds(dz, 1)], tp.at[pl.ds(dz, 1)], tp_send.at[dz], tp_recv.at[dz],
             device(0, 0, dz, 0))
        for dz in FAR
    ]

    partner_copy.wait()
    pairs = lax.broadcasted_iota(jnp.int32, (V, V), 0) + (row * (NY * 2 * NC) + col) * V
    pairs = (pairs == partner_ref[...]).astype(jnp.bfloat16)
    own_unit = ur[pl.ds(0, V), :]
    partner_unit = jnp.dot(pairs, own_unit, preferred_element_type=jnp.float32)
    positive = lax.dot_general(
        ones, own_unit.astype(jnp.float32) * partner_unit, (((1,), (1,)), ((), ())),
        precision=lax.Precision.HIGHEST, preferred_element_type=jnp.float32,
    )[:1] * inv_temp
    rhs[:, pl.ds(0, W)] = ur[...]

    for copy in p_totals:
        copy.wait_recv()
    totals = jnp.sum(tp[...], axis=0)
    tr[0] = totals
    tc[0] = totals
    for rank in range(NY - 1, -1, -1):
        for k in (1, 0):
            for dx in (2, 1, 3, 0):
                slot = (rank * NC + k) * NX + dx
                if slot:
                    remote(tr.at[pl.ds(0, 1)], tr.at[pl.ds(slot, 1)], tr_send, tr_recv,
                           device(-dx, -ORDER[rank], 0, k)).start()
    c_totals = [
        send(tc.at[pl.ds(0, 1)], tc.at[pl.ds(dz, 1)], tc_send.at[dz], tc_recv.at[dz],
             device(0, 0, -dz, 0))
        for dz in FAR
    ]
    losses_ref[...] = jnp.log(totals[:, :V]) - positive

    for copy in c_totals:
        copy.wait_recv()
    inverse = jnp.transpose(1.0 / tc[...].reshape(NZ, W))
    for dz in range(NZ):
        invc[pl.ds(dz * V, V), :] = jnp.broadcast_to(inverse[:V, dz:dz + 1], (V, W))

    rest = remote(tr.at[pl.ds(1, NR - 1)], tr.at[pl.ds(1, NR - 1)], tr_send, tr_recv, (row, col))
    rest.wait_recv()
    inverse = jnp.transpose(1.0 / tr[...].reshape(NR, W))
    for slot in range(NR):
        at = pl.ds(slot * V, V)
        rhs[at, pl.ds(W, W)] = (
            ur[at, :].astype(jnp.float32) * inverse[:V, slot:slot + 1]
        ).astype(jnp.bfloat16)

    outputs = []
    kept = None
    for dz in (4, 2, 6, 0):
        sums = jnp.dot(
            probs[pl.ds(dz * V, 2 * V), :], rhs[...], preferred_element_type=jnp.float32
        )
        part = sums[:, :W] * invc[pl.ds(dz * V, 2 * V), :] + sums[:, W:]
        if dz == 0:
            kept = part[:V]
            sbuf[pl.ds(V, V), :] = part[V:].astype(jnp.bfloat16)
        else:
            sbuf[pl.ds(dz * V, 2 * V), :] = part.astype(jnp.bfloat16)
        for to in (dz, dz + 1):
            if to:
                copy = send(sbuf.at[pl.ds(to * V, V)], rbuf.at[pl.ds(to * V, V)], o_send.at[to],
                            o_recv.at[to], device(0, 0, to, 0))
                outputs.append((to, copy))
    result = kept - 2.0 * partner_unit
    for to, copy in outputs:
        copy.wait_recv()
        result = result + rbuf[pl.ds(to * V, V), :].astype(jnp.float32)
    dunit = result * inv_temp
    proj = proj_ref[...]
    scale = lax.rsqrt(jnp.sum(proj * proj, axis=1, keepdims=True) + epsilon)
    inner = jnp.sum(proj * dunit, axis=1, keepdims=True)
    grad_ref[...] = scale * dunit - scale * scale * scale * proj * inner

    for copy in started:
        copy.wait_send()
    for rank in range(NY):
        share(rank).wait_send()
    rest.wait_send()


def body(projections, partner):
    dma = pltpu.SemaphoreType.DMA
    losses, grad = pl.pallas_call(
        kernel,
        out_shape=(
            jax.ShapeDtypeStruct((1, V), jnp.float32),
            jax.ShapeDtypeStruct((V, W), jnp.float32),
        ),
        in_specs=[pl.BlockSpec(memory_space=pl.ANY)] * 2,
        out_specs=(pl.BlockSpec(memory_space=pltpu.VMEM),) * 2,
        scratch_shapes=[
            pltpu.VMEM((V, W), jnp.float32),
            pltpu.VMEM((1, V), jnp.int32),
            pltpu.VMEM((COLS, W), jnp.bfloat16),
            pltpu.VMEM((ROWS, W), jnp.bfloat16),
            pltpu.VMEM((ROWS, COLS), jnp.bfloat16),
            pltpu.VMEM((ROWS, W), jnp.float32),
            pltpu.VMEM((COLS, 2 * W), jnp.bfloat16),
            pltpu.VMEM((ROWS, W), jnp.float32),
            pltpu.VMEM((NZ, 1, W), jnp.float32),
            pltpu.VMEM((NZ, 1, W), jnp.float32),
            pltpu.VMEM((NR, 1, W), jnp.float32),
            pltpu.VMEM((NZ, 1, W), jnp.float32),
            pltpu.VMEM((ROWS, W), jnp.bfloat16),
            pltpu.VMEM((ROWS, W), jnp.bfloat16),
            dma((2,)), dma((NY, NX)), dma((NY, NX)), dma((NY,)), dma((NY,)), dma((NY,)), dma((NY,)),
            dma((NZ,)), dma((NZ,)), dma((NZ,)), dma((NZ,)), dma, dma, dma((NZ,)), dma((NZ,)),
            dma((NZ,)), dma((NZ,)),
        ],
        compiler_params=pltpu.CompilerParams(
            collective_id=0, has_side_effects=True, vmem_limit_bytes=60 * 1024 * 1024
        ),
    )(projections, partner.reshape(1, V))
    return losses.reshape(V), grad


def solution(mesh):
    in_specs = (P(("row", "col"), None), P(("row", "col")))
    out_specs = (P(("row", "col")), P(("row", "col"), None))
    return jax.shard_map(body, mesh=mesh, in_specs=in_specs, out_specs=out_specs, check_vma=False)
```

```python
import functools

import jax
import jax.numpy as jnp
from jax import lax
from jax.experimental import pallas as pl
from jax.experimental.pallas import tpu as pltpu
from jax.sharding import PartitionSpec as P

inv_temp = 10.0
epsilon = 1e-06
log2e = 1.4426950408889634

V = 96
W = 128
NX, NY, NZ, NC = 4, 8, 8, 2
NR = NX * NY * NC
GROUP = NX * V
BLOCK = NC * GROUP
COLS = NR * V
ROWS = NZ * V
TILE = 256
ORDER = (0, 1, 7, 2, 6, 3, 5, 4)

MESH = pl.DeviceIdType.MESH


def to_rows(tiles):
    rows = []
    for at in range(0, len(tiles), 3):
        first, second, third = tiles[at:at + 3]
        lane = lax.broadcasted_iota(jnp.int32, first.shape, first.ndim - 1)
        turn = functools.partial(pltpu.roll, axis=first.ndim - 1)
        rows.append(first)
        rows.append(jnp.where(lane < 32, turn(first, 32), turn(second, 32)))
        rows.append(jnp.where(lane < 64, turn(second, 64), turn(third, 64)))
        rows.append(turn(third, 96))
    return rows


def to_lanes(rows):
    tiles = []
    for at in range(0, len(rows), 4):
        first, second, third, fourth = rows[at:at + 4]
        lane = lax.broadcasted_iota(jnp.int32, first.shape, first.ndim - 1)
        turn = functools.partial(pltpu.roll, axis=first.ndim - 1)
        second, third, fourth = turn(second, 96), turn(third, 64), turn(fourth, 32)
        tiles.append(jnp.where(lane < 96, first, second))
        tiles.append(jnp.where(lane < 64, second, third))
        tiles.append(jnp.where(lane < 32, third, fourth))
    return tiles


def kernel(
    proj_hbm, partner_hbm, losses_ref, grad_ref,
    proj_ref, partner_ref, ur, cu, probs, acc, ut, uts, plain, tps, tp, to, tr, sbuf, rbuf,
    in_sem, x_send, x_recv, y_send, y_recv, k_send, k_recv, z_send, z_recv,
    tp_send, tp_recv, tr_send, tr_recv, tc_send, tc_recv, o_send, o_recv,
):
    proj_copy = pltpu.make_async_copy(proj_hbm, proj_ref, in_sem.at[0])
    partner_copy = pltpu.make_async_copy(partner_hbm, partner_ref, in_sem.at[1])
    proj_copy.start()
    partner_copy.start()

    row, col = lax.axis_index("row"), lax.axis_index("col")
    z, x_lo = row % NZ, row // NZ
    core, x_hi, y = col % NC, (col // NC) % 2, col // (2 * NC)
    x = x_hi * 2 + x_lo
    at_x = [(x + dx) % NX for dx in range(NX)]
    x_row = [(px % 2) * NZ for px in at_x]
    x_col = [(px // 2) * NC for px in at_x]
    y_col = [((y + dy) % NY) * (2 * NC) for dy in range(NY)]
    at_z = [(z + dz) % NZ for dz in range(NZ)]
    cores = (core, 1 - core)

    def device(dx, dy, dz, dk):
        return (x_row[dx % NX] + at_z[dz % NZ], y_col[dy % NY] + x_col[dx % NX] + cores[dk])

    started = []

    def remote(src, dst, send_sem, recv_sem, to):
        return pltpu.make_async_remote_copy(
            src_ref=src, dst_ref=dst, send_sem=send_sem, recv_sem=recv_sem,
            device_id=to, device_id_type=MESH,
        )

    def send(*args):
        copy = remote(*args)
        copy.start()
        started.append(copy)
        return copy

    barrier = pltpu.get_barrier_semaphore()
    peers = [device(dx, 0, 0, 0) for dx in range(1, NX)]
    peers += [device(0, dy, 0, 0) for dy in range(1, NY)]
    peers += [device(0, 0, dz, 0) for dz in range(1, NZ)]
    peers += [device(0, 0, dz, 1) for dz in range(NZ)]
    for peer in peers:
        pl.semaphore_signal(barrier, inc=1, device_id=peer, device_id_type=MESH)

    tps[...] = jnp.ones_like(tps)
    proj_copy.wait()
    proj = proj_ref[...]
    scale = lax.rsqrt(jnp.sum(proj * proj, axis=1, keepdims=True) + epsilon)
    unit = (proj * scale).astype(jnp.bfloat16)
    ur[pl.ds(0, V), :] = unit
    cu[pl.ds(0, V), :] = unit

    pl.semaphore_wait(barrier, len(peers))

    def block(rank, dx):
        return ur.at[pl.ds(rank * BLOCK + dx * V, V)]

    def to_x(rank, dx):
        return remote(block(rank, 0), block(rank, dx), x_send.at[rank, dx], x_recv.at[rank, dx],
                      device(-dx, 0, 0, 0))

    def pass_on(rank):
        for dx in (1, 3, 2):
            to_x(rank, dx).start()

    def share(rank):
        first = rank * BLOCK
        return remote(ur.at[pl.ds(first, GROUP)], ur.at[pl.ds(first + GROUP, GROUP)],
                      k_send.at[rank], k_recv.at[rank], device(0, 0, 0, 1))

    def share_when_whole(rank):
        for dx in (1, 3, 2):
            to_x(rank, dx).wait_recv()
        share(rank).start()

    def scores(rank, k, diagonal=False):
        first = pl.multiple_of((rank * NC + k) * GROUP, GROUP)
        rows = pl.ds(first, GROUP)
        units = ur[rows, :]
        ut[:, rows] = jnp.transpose(units)
        for lane in range(0, ROWS, TILE):
            lanes = pl.ds(lane, TILE)
            dots = lax.dot_general(
                units, cu[lanes, :], (((1,), (1,)), ((), ())), preferred_element_type=jnp.float32
            )
            values = jnp.exp2(dots * (inv_temp * log2e))
            if diagonal and lane == 0:
                left = lax.broadcasted_iota(jnp.int32, (GROUP, TILE), 0)
                right = lax.broadcasted_iota(jnp.int32, (GROUP, TILE), 1)
                values = jnp.where((left == right) & (left < V), 0.0, values)
            total = jnp.sum(values.reshape(GROUP // 8, 8, TILE), axis=0)
            probs[rows, lanes] = values.astype(jnp.bfloat16)
            if diagonal:
                acc[:, lanes] = total
            else:
                acc[:, lanes] += total

    pass_on(0)
    y_copies, z_copies = [], []
    for rank in range(1, NY):
        y_copies.append(send(block(0, 0), block(rank, 0), y_send.at[rank], y_recv.at[rank],
                             device(0, -ORDER[rank], 0, 0)))
        z_copies.append(send(cu.at[pl.ds(0, V)], cu.at[pl.ds(rank * V, V)], z_send.at[rank],
                             z_recv.at[rank], device(0, 0, -ORDER[rank], 0)))

    def arrived(copies, *ranks):
        for rank in ranks:
            copies[rank - 1].wait_recv()

    for rank in range(1, NY):
        arrived(y_copies, rank)
        pass_on(rank)
    share_when_whole(0)
    arrived(z_copies, *range(1, NZ))
    scores(0, 0, True)

    def own_core(rank, carry):
        share_when_whole(rank)
        scores(rank, 0)
        return carry

    def other_core(rank, carry):
        share(rank).wait_recv()
        scores(rank, 1)
        return carry

    lax.fori_loop(1, NY, own_core, 0)
    lax.fori_loop(0, NY, other_core, 0)

    sums = jnp.sum(acc[...], axis=0, keepdims=True)
    for rank, part in enumerate(to_rows([sums[:, at:at + W] for at in range(0, ROWS, W)])):
        tps[rank] = part
    p_totals = []
    for rank in range(NZ - 1, -1, -1):
        if rank:
            p_totals.append(send(tps, tp.at[rank], tp_send.at[rank], tp_recv.at[rank],
                                 device(0, 0, ORDER[rank], 0)))
        p_totals.append(send(tps.at[pl.ds(rank, 1)], to.at[pl.ds(rank, 1)], tc_send.at[rank],
                             tc_recv.at[rank], device(0, 0, ORDER[rank], 1)))

    partner_copy.wait()
    pairs = lax.broadcasted_iota(jnp.int32, (V, V), 0) + (row * (NY * 2 * NC) + col) * V
    pairs = (pairs == partner_ref[...]).astype(jnp.bfloat16)
    own_unit = ur[pl.ds(0, V), :]
    partner_unit = jnp.dot(pairs, own_unit, preferred_element_type=jnp.float32)
    positive = lax.dot_general(
        jnp.ones((8, W), jnp.float32), own_unit.astype(jnp.float32) * partner_unit, (((1,), (1,)), ((), ())),
        precision=lax.Precision.HIGHEST, preferred_element_type=jnp.float32,
    )[:1] * inv_temp

    def plain_sums(*lanes):
        for lane in lanes:
            plain[:, pl.ds(lane, TILE)] = jnp.dot(
                ut[...], probs[:, pl.ds(lane, TILE)], preferred_element_type=jnp.float32
            )

    plain_sums(0, TILE)
    for copy in p_totals:
        copy.wait_recv()
    where = {offset: rank for rank, offset in enumerate(ORDER)}
    totals_of = []
    for rank in range(NZ):
        total = tps[rank]
        for sender in range(1, NZ):
            total = total + tp[sender, where[(ORDER[rank] + ORDER[sender]) % NZ]]
        totals_of.append(total)
    totals = totals_of[0]
    tr[0] = jnp.concatenate([totals, jnp.sum(to[...], axis=0)], axis=0)
    for rank in range(NY - 1, -1, -1):
        for dx in (2, 1, 3, 0):
            if rank or dx:
                remote(tr.at[pl.ds(0, 1)], tr.at[pl.ds(rank * NX + dx, 1)], tr_send, tr_recv,
                       device(-dx, -ORDER[rank], 0, 0)).start()
    losses_ref[...] = jnp.log(totals[:, :V]) - positive
    inverse = [1.0 / part for part in to_lanes(totals_of)]
    plain_sums(2 * TILE)

    rest = remote(tr.at[pl.ds(1, NX * NY - 1)], tr.at[pl.ds(1, NX * NY - 1)], tr_send, tr_recv,
                  (row, col))
    rest.wait_recv()
    shares_of = tr[...].reshape(NY, NX, NC, W)
    scales = [1.0 / part for part in to_lanes([shares_of[:, dx] for dx in range(NX)])]
    for at in range(0, COLS, W):
        group, tile = at // GROUP, at % GROUP // W
        factor = scales[tile][group // NC, group % NC:group % NC + 1]
        uts[:, pl.ds(at, W)] = (ut[:, pl.ds(at, W)].astype(jnp.float32) * factor).astype(
            jnp.bfloat16
        )

    outputs = []
    for lane in range(ROWS - TILE, -1, -TILE):
        lanes = pl.ds(lane, TILE)
        sums = jnp.dot(uts[...], probs[:, lanes], preferred_element_type=jnp.float32)
        factor = jnp.concatenate(inverse[lane // W:(lane + TILE) // W], axis=1)
        part = jnp.transpose(plain[:, lanes] * factor + sums)
        sbuf[lanes, :] = part.astype(jnp.bfloat16)
        for rank in range(NZ - 1, 0, -1):
            if lane <= rank * V < lane + TILE:
                at = pl.ds(rank * V, V)
                copy = send(sbuf.at[at], rbuf.at[at], o_send.at[rank], o_recv.at[rank],
                            device(0, 0, ORDER[rank], 0))
                outputs.append((rank, copy))
    kept = part[:V]
    result = kept - 2.0 * partner_unit
    for rank, copy in outputs:
        copy.wait_recv()
        result = result + rbuf[pl.ds(rank * V, V), :].astype(jnp.float32)
    dunit = result * inv_temp
    proj = proj_ref[...]
    scale = lax.rsqrt(jnp.sum(proj * proj, axis=1, keepdims=True) + epsilon)
    inner = jnp.sum(proj * dunit, axis=1, keepdims=True)
    grad_ref[...] = scale * dunit - scale * scale * scale * proj * inner

    for copy in started:
        copy.wait_send()
    for rank in range(NY):
        for dx in (1, 3, 2):
            to_x(rank, dx).wait_send()
        share(rank).wait_send()
    rest.wait_send()


def body(projections, partner):
    dma = pltpu.SemaphoreType.DMA
    projections = pltpu.with_memory_space_constraint(projections, pltpu.HBM)
    partner = pltpu.with_memory_space_constraint(partner.reshape(1, V), pltpu.HBM)
    losses, grad = pl.pallas_call(
        kernel,
        out_shape=(pltpu.VMEM((1, V), jnp.float32), pltpu.VMEM((V, W), jnp.float32)),
        in_specs=[pl.BlockSpec(memory_space=pl.ANY)] * 2,
        out_specs=(pl.BlockSpec(memory_space=pltpu.VMEM),) * 2,
        scratch_shapes=[
            pltpu.VMEM((V, W), jnp.float32),
            pltpu.VMEM((1, V), jnp.int32),
            pltpu.VMEM((COLS, W), jnp.bfloat16),
            pltpu.VMEM((ROWS, W), jnp.bfloat16),
            pltpu.VMEM((COLS, ROWS), jnp.bfloat16),
            pltpu.VMEM((8, ROWS), jnp.float32),
            pltpu.VMEM((W, COLS), jnp.bfloat16),
            pltpu.VMEM((W, COLS), jnp.bfloat16),
            pltpu.VMEM((W, ROWS), jnp.float32),
            pltpu.VMEM((NZ, 1, W), jnp.float32),
            pltpu.VMEM((NZ, NZ, 1, W), jnp.float32),
            pltpu.VMEM((NZ, 1, W), jnp.float32),
            pltpu.VMEM((NY * NX, NC, W), jnp.float32),
            pltpu.VMEM((ROWS, W), jnp.bfloat16),
            pltpu.VMEM((ROWS, W), jnp.bfloat16),
            dma((2,)), dma((NY, NX)), dma((NY, NX)), dma((NY,)), dma((NY,)), dma((NY,)), dma((NY,)),
            dma((NZ,)), dma((NZ,)), dma((NZ,)), dma((NZ,)), dma, dma, dma((NZ,)), dma((NZ,)),
            dma((NZ,)), dma((NZ,)),
        ],
        compiler_params=pltpu.CompilerParams(
            collective_id=0, has_side_effects=True, vmem_limit_bytes=48 * 1024 * 1024
        ),
    )(projections, partner)
    return losses.reshape(V), grad


def solution(mesh):
    in_specs = (P(("row", "col"), None), P(("row", "col")))
    out_specs = (P(("row", "col")), P(("row", "col"), None))
    return jax.shard_map(body, mesh=mesh, in_specs=in_specs, out_specs=out_specs, check_vma=False)
```

```python
import functools

import jax
import jax.numpy as jnp
from jax import lax
from jax.experimental import pallas as pl
from jax.experimental.pallas import tpu as pltpu
from jax.sharding import PartitionSpec as P

inv_temp = 10.0
epsilon = 1e-06
log2e = 1.4426950408889634

V = 96
HALF = V // 2
W = 128
NX, NY, NZ, NC = 4, 8, 8, 2
NR = NX * NY * NC
GROUP = NX * V
BLOCK = NC * GROUP
COLS = NR * V
ROWS = NZ * V
TILE = 256
ORDER = (0, 1, 7, 2, 6, 3, 5, 4)

MESH = pl.DeviceIdType.MESH


def to_rows(tiles):
    rows = []
    for at in range(0, len(tiles), 3):
        first, second, third = tiles[at:at + 3]
        lane = lax.broadcasted_iota(jnp.int32, first.shape, first.ndim - 1)
        turn = functools.partial(pltpu.roll, axis=first.ndim - 1)
        rows.append(first)
        rows.append(jnp.where(lane < 32, turn(first, 32), turn(second, 32)))
        rows.append(jnp.where(lane < 64, turn(second, 64), turn(third, 64)))
        rows.append(turn(third, 96))
    return rows


def to_lanes(rows):
    tiles = []
    for at in range(0, len(rows), 4):
        first, second, third, fourth = rows[at:at + 4]
        lane = lax.broadcasted_iota(jnp.int32, first.shape, first.ndim - 1)
        turn = functools.partial(pltpu.roll, axis=first.ndim - 1)
        second, third, fourth = turn(second, 96), turn(third, 64), turn(fourth, 32)
        tiles.append(jnp.where(lane < 96, first, second))
        tiles.append(jnp.where(lane < 64, second, third))
        tiles.append(jnp.where(lane < 32, third, fourth))
    return tiles


def kernel(
    proj_hbm, partner_hbm, losses_ref, grad_ref,
    proj_ref, partner_ref, ur, cu, probs, acc, both, tps, tp, to, tr, sbuf, rbuf,
    in_sem, x_send, x_recv, y_send, y_recv, f_send, f_recv, k_send, k_recv, z_send, z_recv,
    tp_send, tp_recv, tr_send, tr_recv, tc_send, tc_recv, o_send, o_recv,
):
    proj_copy = pltpu.make_async_copy(proj_hbm, proj_ref, in_sem.at[0])
    partner_copy = pltpu.make_async_copy(partner_hbm, partner_ref, in_sem.at[1])
    proj_copy.start()
    partner_copy.start()

    row, col = lax.axis_index("row"), lax.axis_index("col")
    z, x_lo = row % NZ, row // NZ
    core, x_hi, y = col % NC, (col // NC) % 2, col // (2 * NC)
    x = x_hi * 2 + x_lo
    at_x = [(x + dx) % NX for dx in range(NX)]
    x_row = [(px % 2) * NZ for px in at_x]
    x_col = [(px // 2) * NC for px in at_x]
    y_col = [((y + dy) % NY) * (2 * NC) for dy in range(NY)]
    at_z = [(z + dz) % NZ for dz in range(NZ)]
    cores = (core, 1 - core)

    def device(dx, dy, dz, dk):
        return (x_row[dx % NX] + at_z[dz % NZ], y_col[dy % NY] + x_col[dx % NX] + cores[dk])

    started = []

    def remote(src, dst, send_sem, recv_sem, to):
        return pltpu.make_async_remote_copy(
            src_ref=src, dst_ref=dst, send_sem=send_sem, recv_sem=recv_sem,
            device_id=to, device_id_type=MESH,
        )

    def send(*args):
        copy = remote(*args)
        copy.start()
        started.append(copy)
        return copy

    barrier = pltpu.get_barrier_semaphore()
    peers = [device(dx, 0, 0, 0) for dx in range(1, NX)]
    peers += [device(0, dy, 0, 0) for dy in range(1, NY)]
    peers += [device(0, 0, dz, 0) for dz in range(1, NZ)]
    peers += [device(0, 0, dz, 1) for dz in range(NZ)]
    for peer in peers:
        pl.semaphore_signal(barrier, inc=1, device_id=peer, device_id_type=MESH)

    tps[...] = jnp.ones_like(tps)
    proj_copy.wait()
    proj = proj_ref[...]
    scale = lax.rsqrt(jnp.sum(proj * proj, axis=1, keepdims=True) + epsilon)
    unit = (proj * scale).astype(jnp.bfloat16)
    ur[pl.ds(0, V), :] = unit
    cu[pl.ds(0, V), :] = unit

    pl.semaphore_wait(barrier, len(peers))

    def block(rank, dx, half=None):
        first = rank * BLOCK + dx * V
        return ur.at[pl.ds(first, V)] if half is None else ur.at[pl.ds(first + half * HALF, HALF)]

    def to_x(rank, dx):
        half = 1 if dx == 2 and not (isinstance(rank, int) and rank == 0) else None
        return remote(block(rank, 0, half), block(rank, dx, half), x_send.at[rank, dx],
                      x_recv.at[rank, dx], device(-dx, 0, 0, 0))

    def from_far(rank):
        dy = ORDER[rank] if isinstance(rank, int) else 1
        return remote(block(0, 2, 0), block(rank, 2, 0), f_send.at[rank], f_recv.at[rank],
                      device(0, -dy, 0, 0))

    def pass_on(rank):
        for dx in (1, 3, 2):
            to_x(rank, dx).start()

    def share(rank):
        first = rank * BLOCK
        return remote(ur.at[pl.ds(first, GROUP)], ur.at[pl.ds(first + GROUP, GROUP)],
                      k_send.at[rank], k_recv.at[rank], device(0, 0, 0, 1))

    def share_when_whole(rank):
        for dx in (1, 3) if isinstance(rank, int) and rank == 0 else (1, 3, 2):
            to_x(rank, dx).wait_recv()
        if not (isinstance(rank, int) and rank == 0):
            from_far(rank).wait_recv()
        share(rank).start()

    def scores(rank, k, diagonal=False):
        first = pl.multiple_of((rank * NC + k) * GROUP, GROUP)
        rows = pl.ds(first, GROUP)
        units = ur[rows, :]
        both[pl.ds(0, W), rows] = jnp.transpose(units)
        for lane in range(0, ROWS, TILE):
            lanes = pl.ds(lane, TILE)
            dots = lax.dot_general(
                units, cu[lanes, :], (((1,), (1,)), ((), ())), preferred_element_type=jnp.float32
            )
            values = jnp.exp2(dots * (inv_temp * log2e))
            if diagonal and lane == 0:
                left = lax.broadcasted_iota(jnp.int32, (GROUP, TILE), 0)
                right = lax.broadcasted_iota(jnp.int32, (GROUP, TILE), 1)
                values = jnp.where((left == right) & (left < V), 0.0, values)
            total = jnp.sum(values.reshape(GROUP // 8, 8, TILE), axis=0)
            probs[rows, lanes] = values.astype(jnp.bfloat16)
            if diagonal:
                acc[:, lanes] = total
            else:
                acc[:, lanes] += total

    pass_on(0)
    y_copies, z_copies = [], []
    for rank in range(1, NY):
        y_copies.append(send(block(0, 0), block(rank, 0), y_send.at[rank], y_recv.at[rank],
                             device(0, -ORDER[rank], 0, 0)))
        z_copies.append(send(cu.at[pl.ds(0, V)], cu.at[pl.ds(rank * V, V)], z_send.at[rank],
                             z_recv.at[rank], device(0, 0, -ORDER[rank], 0)))

    def arrived(copies, *ranks):
        for rank in ranks:
            copies[rank - 1].wait_recv()

    arrived(y_copies, 1)
    pass_on(1)
    arrived(y_copies, 2)
    pass_on(2)
    to_x(0, 2).wait_recv()
    for rank in range(1, NY):
        from_far(rank).start()
    for rank in range(3, NY):
        arrived(y_copies, rank)
        pass_on(rank)
    share_when_whole(0)
    arrived(z_copies, *range(1, NZ))
    scores(0, 0, True)

    def own_core(rank, carry):
        share_when_whole(rank)
        scores(rank, 0)
        return carry

    def other_core(rank, carry):
        share(rank).wait_recv()
        scores(rank, 1)
        return carry

    def both_cores(rank, carry):
        own_core(rank, carry)
        other_core(rank - 2, carry)
        return carry

    own_core(1, 0)
    lax.fori_loop(2, NY, both_cores, 0)
    lax.fori_loop(NY - 2, NY, other_core, 0)

    sums = jnp.sum(acc[...], axis=0, keepdims=True)
    for rank, part in enumerate(to_rows([sums[:, at:at + W] for at in range(0, ROWS, W)])):
        tps[rank] = part
    p_totals = []
    for rank in range(NZ - 1, -1, -1):
        if rank:
            p_totals.append(send(tps, tp.at[rank], tp_send.at[rank], tp_recv.at[rank],
                                 device(0, 0, ORDER[rank], 0)))
        p_totals.append(send(tps.at[pl.ds(rank, 1)], to.at[pl.ds(rank, 1)], tc_send.at[rank],
                             tc_recv.at[rank], device(0, 0, ORDER[rank], 1)))

    partner_copy.wait()
    pairs = lax.broadcasted_iota(jnp.int32, (V, V), 0) + (row * (NY * 2 * NC) + col) * V
    pairs = (pairs == partner_ref[...]).astype(jnp.bfloat16)
    own_unit = ur[pl.ds(0, V), :]
    partner_unit = jnp.dot(pairs, own_unit, preferred_element_type=jnp.float32)
    positive = lax.dot_general(
        jnp.ones((8, W), jnp.float32), own_unit.astype(jnp.float32) * partner_unit, (((1,), (1,)), ((), ())),
        precision=lax.Precision.HIGHEST, preferred_element_type=jnp.float32,
    )[:1] * inv_temp

    for copy in p_totals:
        copy.wait_recv()
    where = {offset: rank for rank, offset in enumerate(ORDER)}
    totals_of = []
    for rank in range(NZ):
        total = tps[rank]
        for sender in range(1, NZ):
            total = total + tp[sender, where[(ORDER[rank] + ORDER[sender]) % NZ]]
        totals_of.append(total)
    totals = totals_of[0]
    tr[0] = jnp.concatenate([totals, jnp.sum(to[...], axis=0)], axis=0)
    for rank in range(NY - 1, -1, -1):
        for dx in (2, 1, 3, 0):
            if rank or dx:
                remote(tr.at[pl.ds(0, 1)], tr.at[pl.ds(rank * NX + dx, 1)], tr_send, tr_recv,
                       device(-dx, -ORDER[rank], 0, 0)).start()
    losses_ref[...] = jnp.log(totals[:, :V]) - positive
    inverse = [1.0 / part for part in to_lanes(totals_of)]

    rest = remote(tr.at[pl.ds(1, NX * NY - 1)], tr.at[pl.ds(1, NX * NY - 1)], tr_send, tr_recv,
                  (row, col))
    rest.wait_recv()
    shares_of = tr[...].reshape(NY, NX, NC, W)
    scales = [1.0 / part for part in to_lanes([shares_of[:, dx] for dx in range(NX)])]
    for at in range(0, COLS, W):
        group, tile = at // GROUP, at % GROUP // W
        factor = scales[tile][group // NC, group % NC:group % NC + 1]
        both[pl.ds(W, W), pl.ds(at, W)] = (
            both[pl.ds(0, W), pl.ds(at, W)].astype(jnp.float32) * factor
        ).astype(jnp.bfloat16)

    outputs = []
    for lane in range(ROWS - TILE, -1, -TILE):
        lanes = pl.ds(lane, TILE)
        sums = jnp.dot(both[...], probs[:, lanes], preferred_element_type=jnp.float32)
        factor = jnp.concatenate(inverse[lane // W:(lane + TILE) // W], axis=1)
        part = jnp.transpose(sums[:W] * factor + sums[W:])
        sbuf[lanes, :] = part.astype(jnp.bfloat16)
        for rank in range(NZ - 1, 0, -1):
            if lane <= rank * V < lane + TILE:
                at = pl.ds(rank * V, V)
                copy = send(sbuf.at[at], rbuf.at[at], o_send.at[rank], o_recv.at[rank],
                            device(0, 0, ORDER[rank], 0))
                outputs.append((rank, copy))
    kept = part[:V]
    result = kept - 2.0 * partner_unit
    for rank, copy in outputs:
        copy.wait_recv()
        result = result + rbuf[pl.ds(rank * V, V), :].astype(jnp.float32)
    dunit = result * inv_temp
    proj = proj_ref[...]
    scale = lax.rsqrt(jnp.sum(proj * proj, axis=1, keepdims=True) + epsilon)
    inner = jnp.sum(proj * dunit, axis=1, keepdims=True)
    grad_ref[...] = scale * dunit - scale * scale * scale * proj * inner

    for copy in started:
        copy.wait_send()
    for rank in range(NY):
        for dx in (1, 3, 2):
            to_x(rank, dx).wait_send()
        if rank:
            from_far(rank).wait_send()
        share(rank).wait_send()
    rest.wait_send()


def body(projections, partner):
    dma = pltpu.SemaphoreType.DMA
    projections = pltpu.with_memory_space_constraint(projections, pltpu.HBM)
    partner = pltpu.with_memory_space_constraint(partner.reshape(1, V), pltpu.HBM)
    losses, grad = pl.pallas_call(
        kernel,
        out_shape=(pltpu.VMEM((1, V), jnp.float32), pltpu.VMEM((V, W), jnp.float32)),
        in_specs=[pl.BlockSpec(memory_space=pl.ANY)] * 2,
        out_specs=(pl.BlockSpec(memory_space=pltpu.VMEM),) * 2,
        scratch_shapes=[
            pltpu.VMEM((V, W), jnp.float32),
            pltpu.VMEM((1, V), jnp.int32),
            pltpu.VMEM((COLS, W), jnp.bfloat16),
            pltpu.VMEM((ROWS, W), jnp.bfloat16),
            pltpu.VMEM((COLS, ROWS), jnp.bfloat16),
            pltpu.VMEM((8, ROWS), jnp.float32),
            pltpu.VMEM((2 * W, COLS), jnp.bfloat16),
            pltpu.VMEM((NZ, 1, W), jnp.float32),
            pltpu.VMEM((NZ, NZ, 1, W), jnp.float32),
            pltpu.VMEM((NZ, 1, W), jnp.float32),
            pltpu.VMEM((NY * NX, NC, W), jnp.float32),
            pltpu.VMEM((ROWS, W), jnp.bfloat16),
            pltpu.VMEM((ROWS, W), jnp.bfloat16),
            dma((2,)), dma((NY, NX)), dma((NY, NX)), dma((NY,)), dma((NY,)), dma((NY,)), dma((NY,)),
            dma((NY,)), dma((NY,)),
            dma((NZ,)), dma((NZ,)), dma((NZ,)), dma((NZ,)), dma, dma, dma((NZ,)), dma((NZ,)),
            dma((NZ,)), dma((NZ,)),
        ],
        compiler_params=pltpu.CompilerParams(
            collective_id=0, has_side_effects=True, vmem_limit_bytes=48 * 1024 * 1024
        ),
    )(projections, partner)
    return losses.reshape(V), grad


def solution(mesh):
    in_specs = (P(("row", "col"), None), P(("row", "col")))
    out_specs = (P(("row", "col")), P(("row", "col"), None))
    return jax.shard_map(body, mesh=mesh, in_specs=in_specs, out_specs=out_specs, check_vma=False)
```

```python
import functools

import jax
import jax.numpy as jnp
from jax import lax
from jax.experimental import pallas as pl
from jax.experimental.pallas import tpu as pltpu
from jax.sharding import PartitionSpec as P

inv_temp = 10.0
epsilon = 1e-06
log2e = 1.4426950408889634

V = 96
W = 128
NX, NY, NZ, NC = 4, 8, 8, 2
GROUP = NX * V
ROWS = NY * GROUP
HALF = NZ * V
COLS = NC * HALF
TILE = 256
ORDER = (0, 1, 7, 2, 6, 3, 5, 4)

MESH = pl.DeviceIdType.MESH


def to_rows(tiles):
    rows = []
    for at in range(0, len(tiles), 3):
        first, second, third = tiles[at:at + 3]
        lane = lax.broadcasted_iota(jnp.int32, first.shape, first.ndim - 1)
        turn = functools.partial(pltpu.roll, axis=first.ndim - 1)
        rows.append(first)
        rows.append(jnp.where(lane < 32, turn(first, 32), turn(second, 32)))
        rows.append(jnp.where(lane < 64, turn(second, 64), turn(third, 64)))
        rows.append(turn(third, 96))
    return rows


def to_lanes(rows):
    tiles = []
    for at in range(0, len(rows), 4):
        first, second, third, fourth = rows[at:at + 4]
        lane = lax.broadcasted_iota(jnp.int32, first.shape, first.ndim - 1)
        turn = functools.partial(pltpu.roll, axis=first.ndim - 1)
        second, third, fourth = turn(second, 96), turn(third, 64), turn(fourth, 32)
        tiles.append(jnp.where(lane < 96, first, second))
        tiles.append(jnp.where(lane < 64, second, third))
        tiles.append(jnp.where(lane < 32, third, fourth))
    return tiles


def kernel(
    proj_hbm, partner_hbm, losses_ref, grad_ref,
    proj_ref, partner_ref, ur, cu, cut, probs, acc, both, tps, tp, tr, sbuf, rbuf, kbuf, mbuf,
    in_sem, x_send, x_recv, y_send, y_recv, k_send, k_recv, z_send, z_recv,
    tp_send, tp_recv, tr_send, tr_recv, o_send, o_recv, m_send, m_recv,
):
    proj_copy = pltpu.make_async_copy(proj_hbm, proj_ref, in_sem.at[0])
    partner_copy = pltpu.make_async_copy(partner_hbm, partner_ref, in_sem.at[1])
    proj_copy.start()
    partner_copy.start()

    row, col = lax.axis_index("row"), lax.axis_index("col")
    z, x_lo = row % NZ, row // NZ
    core, x_hi, y = col % NC, (col // NC) % 2, col // (2 * NC)
    x = x_hi * 2 + x_lo
    at_x = [(x + dx) % NX for dx in range(NX)]
    x_row = [(px % 2) * NZ for px in at_x]
    x_col = [(px // 2) * NC for px in at_x]
    y_col = [((y + dy) % NY) * (2 * NC) for dy in range(NY)]
    at_z = [(z + dz) % NZ for dz in range(NZ)]
    cores = (core, 1 - core)

    def device(dx, dy, dz, dk):
        return (x_row[dx % NX] + at_z[dz % NZ], y_col[dy % NY] + x_col[dx % NX] + cores[dk])

    started = []

    def remote(src, dst, send_sem, recv_sem, to):
        return pltpu.make_async_remote_copy(
            src_ref=src, dst_ref=dst, send_sem=send_sem, recv_sem=recv_sem,
            device_id=to, device_id_type=MESH,
        )

    def send(*args):
        copy = remote(*args)
        copy.start()
        started.append(copy)
        return copy

    barrier = pltpu.get_barrier_semaphore()
    peers = [device(dx, 0, 0, 0) for dx in range(1, NX)]
    peers += [device(0, dy, 0, 0) for dy in range(1, NY)]
    peers += [device(0, 0, dz, 0) for dz in range(1, NZ)]
    peers += [device(0, 0, dz, 1) for dz in range(NZ)]
    for peer in peers:
        pl.semaphore_signal(barrier, inc=1, device_id=peer, device_id_type=MESH)

    tps[...] = jnp.ones_like(tps)
    proj_copy.wait()
    proj = proj_ref[...]
    scale = lax.rsqrt(jnp.sum(proj * proj, axis=1, keepdims=True) + epsilon)
    unit = (proj * scale).astype(jnp.bfloat16)
    ur[pl.ds(0, V), :] = unit
    cu[pl.ds(0, V), :] = unit

    pl.semaphore_wait(barrier, len(peers))

    def block(rank, dx):
        return ur.at[pl.ds(rank * GROUP + dx * V, V)]

    def to_x(rank, dx):
        return remote(block(rank, 0), block(rank, dx), x_send.at[rank, dx], x_recv.at[rank, dx],
                      device(-dx, 0, 0, 0))

    def pass_on(rank):
        for dx in (1, 3, 2):
            to_x(rank, dx).start()

    def whole(rank):
        for dx in (1, 3, 2):
            to_x(rank, dx).wait_recv()

    def turned(lane):
        cut[:, pl.ds(lane, TILE)] = jnp.transpose(cu[pl.ds(lane, TILE), :])

    def scores(rank, tiles, fresh=False):
        first = pl.multiple_of(rank * GROUP, GROUP)
        rows = pl.ds(first, GROUP)
        units = ur[rows, :]
        if 0 in tiles:
            both[pl.ds(0, W), rows] = jnp.transpose(units)
        for lane in tiles:
            lanes = pl.ds(lane, TILE)
            dots = jnp.dot(units, cut[:, lanes], preferred_element_type=jnp.float32)
            values = jnp.exp2(dots * (inv_temp * log2e))
            if fresh and lane == 0:
                left = lax.broadcasted_iota(jnp.int32, (GROUP, TILE), 0)
                right = lax.broadcasted_iota(jnp.int32, (GROUP, TILE), 1)
                values = jnp.where((left == right) & (left < V), 0.0, values)
            total = jnp.sum(values.reshape(GROUP // 8, 8, TILE), axis=0)
            probs[rows, lanes] = values.astype(jnp.bfloat16)
            if fresh:
                acc[:, lanes] = total
            else:
                acc[:, lanes] += total

    pass_on(0)
    y_copies, z_copies = [], []
    for rank in range(1, NY):
        y_copies.append(send(block(0, 0), block(rank, 0), y_send.at[rank], y_recv.at[rank],
                             device(0, -ORDER[rank], 0, 0)))
        z_copies.append(send(cu.at[pl.ds(0, V)], cu.at[pl.ds(rank * V, V)], z_send.at[rank],
                             z_recv.at[rank], device(0, 0, -ORDER[rank], 0)))

    def arrived(copies, *ranks):
        for rank in ranks:
            copies[rank - 1].wait_recv()

    def go_on(*ranks):
        for rank in ranks:
            arrived(y_copies, rank)
            pass_on(rank)

    go_on(1, 2)
    arrived(z_copies, 1, 2)
    turned(0)
    whole(0)
    scores(0, (0,), True)
    go_on(3, 4)
    arrived(z_copies, 3, 4, 5)
    turned(TILE)
    go_on(5, 6)
    arrived(z_copies, 6, 7)
    other = send(cu.at[pl.ds(0, HALF)], cu.at[pl.ds(HALF, HALF)], k_send, k_recv,
                 device(0, 0, 0, 1))
    go_on(7)
    turned(2 * TILE)
    scores(0, (TILE, 2 * TILE), True)
    whole(1)
    scores(1, range(0, HALF, TILE))
    other.wait_recv()
    for lane in range(HALF, COLS, TILE):
        turned(lane)
    scores(0, range(HALF, COLS, TILE), True)
    scores(1, range(HALF, COLS, TILE))

    def step(rank, carry):
        whole(rank)
        scores(rank, range(0, COLS, TILE))
        return carry

    lax.fori_loop(2, NY, step, 0)

    sums = jnp.sum(acc[...], axis=0, keepdims=True)
    for rank, part in enumerate(to_rows([sums[:, at:at + W] for at in range(0, COLS, W)])):
        tps[rank] = part
    p_totals = []
    for rank in range(NZ - 1, -1, -1):
        for k in (0, 1):
            if rank or k:
                at = k * NZ + rank
                p_totals.append(send(tps, tp.at[at], tp_send.at[at], tp_recv.at[at],
                                     device(0, 0, ORDER[rank], k)))

    partner_copy.wait()
    pairs = lax.broadcasted_iota(jnp.int32, (V, V), 0) + (row * (NY * 2 * NC) + col) * V
    pairs = (pairs == partner_ref[...]).astype(jnp.bfloat16)
    own_unit = ur[pl.ds(0, V), :]
    partner_unit = jnp.dot(pairs, own_unit, preferred_element_type=jnp.float32)
    positive = lax.dot_general(
        jnp.ones((8, W), jnp.float32), own_unit.astype(jnp.float32) * partner_unit, (((1,), (1,)), ((), ())),
        precision=lax.Precision.HIGHEST, preferred_element_type=jnp.float32,
    )[:1] * inv_temp

    for copy in p_totals:
        copy.wait_recv()
    where = {offset: rank for rank, offset in enumerate(ORDER)}
    totals_of = []
    totals_of = []
    for k in range(NC):
        for rank in range(NZ):
            total = tps[k * NZ + rank]
            for sender in range(1, NC * NZ):
                there = where[(ORDER[rank] + ORDER[sender % NZ]) % NZ]
                total = total + tp[sender, (k + sender // NZ) % NC * NZ + there]
            totals_of.append(total)
    totals = totals_of[0]
    tr[0] = totals
    for rank in range(NY - 1, -1, -1):
        for dx in (2, 1, 3, 0):
            if rank or dx:
                remote(tr.at[pl.ds(0, 1)], tr.at[pl.ds(rank * NX + dx, 1)], tr_send, tr_recv,
                       device(-dx, -ORDER[rank], 0, 0)).start()
    losses_ref[...] = jnp.log(totals[:, :V]) - positive
    inverse = [1.0 / part for part in to_lanes(totals_of)]

    rest = remote(tr.at[pl.ds(1, NX * NY - 1)], tr.at[pl.ds(1, NX * NY - 1)], tr_send, tr_recv,
                  (row, col))
    rest.wait_recv()
    shares_of = tr[...].reshape(NY, NX, 1, W)
    scales = [1.0 / part for part in to_lanes([shares_of[:, dx] for dx in range(NX)])]
    for at in range(0, ROWS, W):
        factor = scales[at % GROUP // W][at // GROUP]
        both[pl.ds(W, W), pl.ds(at, W)] = (
            both[pl.ds(0, W), pl.ds(at, W)].astype(jnp.float32) * factor
        ).astype(jnp.bfloat16)

    def parts(lane):
        sums = jnp.dot(both[...], probs[:, pl.ds(lane, TILE)], preferred_element_type=jnp.float32)
        factor = jnp.concatenate(inverse[lane // W:(lane + TILE) // W], axis=1)
        return jnp.transpose(sums[:W] * factor + sums[W:])

    added = {}
    for lane in range(HALF - TILE, -1, -TILE):
        at = pl.ds(lane, TILE)
        kbuf[at, :] = parts(HALF + lane).astype(jnp.bfloat16)
        added[lane] = send(kbuf.at[at], mbuf.at[at], m_send.at[lane // TILE],
                           m_recv.at[lane // TILE], device(0, 0, 0, 1))

    outputs = []
    for lane in range(HALF - TILE, -1, -TILE):
        lanes = pl.ds(lane, TILE)
        part = parts(lane)
        added[lane].wait_recv()
        part = part + mbuf[lanes, :].astype(jnp.float32)
        sbuf[lanes, :] = part.astype(jnp.bfloat16)
        for rank in range(NZ - 1, 0, -1):
            if lane <= rank * V < lane + TILE:
                at = pl.ds(rank * V, V)
                copy = send(sbuf.at[at], rbuf.at[at], o_send.at[rank], o_recv.at[rank],
                            device(0, 0, ORDER[rank], 0))
                outputs.append((rank, copy))
    kept = part[:V]
    result = kept - 2.0 * partner_unit
    for rank, copy in outputs:
        copy.wait_recv()
        result = result + rbuf[pl.ds(rank * V, V), :].astype(jnp.float32)
    dunit = result * inv_temp
    proj = proj_ref[...]
    scale = lax.rsqrt(jnp.sum(proj * proj, axis=1, keepdims=True) + epsilon)
    inner = jnp.sum(proj * dunit, axis=1, keepdims=True)
    grad_ref[...] = scale * dunit - scale * scale * scale * proj * inner

    for copy in started:
        copy.wait_send()
    for rank in range(NY):
        for dx in (1, 3, 2):
            to_x(rank, dx).wait_send()
    rest.wait_send()


def body(projections, partner):
    dma = pltpu.SemaphoreType.DMA
    projections = pltpu.with_memory_space_constraint(projections, pltpu.HBM)
    partner = pltpu.with_memory_space_constraint(partner.reshape(1, V), pltpu.HBM)
    losses, grad = pl.pallas_call(
        kernel,
        out_shape=(pltpu.VMEM((1, V), jnp.float32), pltpu.VMEM((V, W), jnp.float32)),
        in_specs=[pl.BlockSpec(memory_space=pl.ANY)] * 2,
        out_specs=(pl.BlockSpec(memory_space=pltpu.VMEM),) * 2,
        scratch_shapes=[
            pltpu.VMEM((V, W), jnp.float32),
            pltpu.VMEM((1, V), jnp.int32),
            pltpu.VMEM((ROWS, W), jnp.bfloat16),
            pltpu.VMEM((COLS, W), jnp.bfloat16),
            pltpu.VMEM((W, COLS), jnp.bfloat16),
            pltpu.VMEM((ROWS, COLS), jnp.bfloat16),
            pltpu.VMEM((8, COLS), jnp.float32),
            pltpu.VMEM((2 * W, ROWS), jnp.bfloat16),
            pltpu.VMEM((NC * NZ, 1, W), jnp.float32),
            pltpu.VMEM((NC * NZ, NC * NZ, 1, W), jnp.float32),
            pltpu.VMEM((NX * NY, 1, W), jnp.float32),
            pltpu.VMEM((HALF, W), jnp.bfloat16),
            pltpu.VMEM((HALF, W), jnp.bfloat16),
            pltpu.VMEM((HALF, W), jnp.bfloat16),
            pltpu.VMEM((HALF, W), jnp.bfloat16),
            dma((2,)), dma((NY, NX)), dma((NY, NX)), dma((NY,)), dma((NY,)), dma, dma,
            dma((NZ,)), dma((NZ,)), dma((NC * NZ,)), dma((NC * NZ,)), dma, dma, dma((NZ,)), dma((NZ,)),
            dma((HALF // TILE,)), dma((HALF // TILE,)),
        ],
        compiler_params=pltpu.CompilerParams(
            collective_id=0, has_side_effects=True, vmem_limit_bytes=48 * 1024 * 1024
        ),
    )(projections, partner)
    return losses.reshape(V), grad


def solution(mesh):
    in_specs = (P(("row", "col"), None), P(("row", "col")))
    out_specs = (P(("row", "col")), P(("row", "col"), None))
    return jax.shard_map(body, mesh=mesh, in_specs=in_specs, out_specs=out_specs, check_vma=False)
```

```python
import functools

import jax
import jax.numpy as jnp
from jax import lax
from jax.experimental import pallas as pl
from jax.experimental.pallas import tpu as pltpu
from jax.sharding import PartitionSpec as P

inv_temp = 10.0
epsilon = 1e-06
log2e = 1.4426950408889634

V = 96
W = 128
NX, NY, NZ, NC = 4, 8, 8, 2
NR = NX * NY * NC
GROUP = NX * V
BLOCK = NC * GROUP
COLS = NR * V
ROWS = NZ * V
TILE = 256
ORDER = (0, 1, 7, 2, 6, 3, 5, 4)

MESH = pl.DeviceIdType.MESH


def to_rows(tiles):
    rows = []
    for at in range(0, len(tiles), 3):
        first, second, third = tiles[at:at + 3]
        lane = lax.broadcasted_iota(jnp.int32, first.shape, first.ndim - 1)
        turn = functools.partial(pltpu.roll, axis=first.ndim - 1)
        rows.append(first)
        rows.append(jnp.where(lane < 32, turn(first, 32), turn(second, 32)))
        rows.append(jnp.where(lane < 64, turn(second, 64), turn(third, 64)))
        rows.append(turn(third, 96))
    return rows


def to_lanes(rows):
    tiles = []
    for at in range(0, len(rows), 4):
        first, second, third, fourth = rows[at:at + 4]
        lane = lax.broadcasted_iota(jnp.int32, first.shape, first.ndim - 1)
        turn = functools.partial(pltpu.roll, axis=first.ndim - 1)
        second, third, fourth = turn(second, 96), turn(third, 64), turn(fourth, 32)
        tiles.append(jnp.where(lane < 96, first, second))
        tiles.append(jnp.where(lane < 64, second, third))
        tiles.append(jnp.where(lane < 32, third, fourth))
    return tiles


def kernel(
    proj_hbm, partner_hbm, losses_ref, grad_ref,
    proj_ref, partner_ref, ur, cu, probs, acc, ut, uts, plain, tps, tp, to, tr, sbuf, rbuf,
    in_sem, x_send, x_recv, y_send, y_recv, k_send, k_recv, z_send, z_recv,
    tp_send, tp_recv, tr_send, tr_recv, tc_send, tc_recv, o_send, o_recv,
):
    proj_copy = pltpu.make_async_copy(proj_hbm, proj_ref, in_sem.at[0])
    partner_copy = pltpu.make_async_copy(partner_hbm, partner_ref, in_sem.at[1])
    proj_copy.start()
    partner_copy.start()

    row, col = lax.axis_index("row"), lax.axis_index("col")
    z, x_lo = row % NZ, row // NZ
    core, x_hi, y = col % NC, (col // NC) % 2, col // (2 * NC)
    x = x_hi * 2 + x_lo
    at_x = [(x + dx) % NX for dx in range(NX)]
    x_row = [(px % 2) * NZ for px in at_x]
    x_col = [(px // 2) * NC for px in at_x]
    y_col = [((y + dy) % NY) * (2 * NC) for dy in range(NY)]
    at_z = [(z + dz) % NZ for dz in range(NZ)]
    cores = (core, 1 - core)

    def device(dx, dy, dz, dk):
        return (x_row[dx % NX] + at_z[dz % NZ], y_col[dy % NY] + x_col[dx % NX] + cores[dk])

    started = []

    def remote(src, dst, send_sem, recv_sem, to):
        return pltpu.make_async_remote_copy(
            src_ref=src, dst_ref=dst, send_sem=send_sem, recv_sem=recv_sem,
            device_id=to, device_id_type=MESH,
        )

    def send(*args):
        copy = remote(*args)
        copy.start()
        started.append(copy)
        return copy

    barrier = pltpu.get_barrier_semaphore()
    peers = [device(dx, 0, 0, 0) for dx in range(1, NX)]
    peers += [device(0, dy, 0, 0) for dy in range(1, NY)]
    peers += [device(0, 0, dz, 0) for dz in range(1, NZ)]
    peers += [device(0, 0, 0, 1)]
    for peer in peers:
        pl.semaphore_signal(barrier, inc=1, device_id=peer, device_id_type=MESH)

    tps[...] = jnp.ones_like(tps)
    proj_copy.wait()
    proj = proj_ref[...]
    scale = lax.rsqrt(jnp.sum(proj * proj, axis=1, keepdims=True) + epsilon)
    unit = (proj * scale).astype(jnp.bfloat16)
    ur[pl.ds(0, V), :] = unit
    cu[pl.ds(0, V), :] = unit

    pl.semaphore_wait(barrier, len(peers))

    def block(rank, dx):
        return ur.at[pl.ds(rank * BLOCK + dx * V, V)]

    def to_x(rank, dx):
        return remote(block(rank, 0), block(rank, dx), x_send.at[rank, dx], x_recv.at[rank, dx],
                      device(-dx, 0, 0, 0))

    def pass_on(rank):
        for dx in (1, 3, 2):
            to_x(rank, dx).start()

    def share(rank):
        first = rank * BLOCK
        return remote(ur.at[pl.ds(first, GROUP)], ur.at[pl.ds(first + GROUP, GROUP)],
                      k_send.at[rank], k_recv.at[rank], device(0, 0, 0, 1))

    def share_when_whole(rank):
        for dx in (1, 3, 2):
            to_x(rank, dx).wait_recv()
        share(rank).start()

    def scores(rank, diagonal=False):
        first = pl.multiple_of(rank * BLOCK, BLOCK)
        ut[:, pl.ds(first, BLOCK)] = jnp.transpose(ur[pl.ds(first, BLOCK), :])
        for lane in range(0, ROWS, TILE):
            lanes = pl.ds(lane, TILE)
            others = cu[lanes, :]
            total = None
            for at in range(0, BLOCK, TILE):
                rows = pl.ds(first + at, TILE)
                dots = lax.dot_general(
                    ur[rows, :], others, (((1,), (1,)), ((), ())),
                    preferred_element_type=jnp.float32,
                )
                values = jnp.exp2(dots * (inv_temp * log2e))
                if diagonal and lane == 0 and at == 0:
                    left = lax.broadcasted_iota(jnp.int32, (TILE, TILE), 0)
                    right = lax.broadcasted_iota(jnp.int32, (TILE, TILE), 1)
                    values = jnp.where((left == right) & (left < V), 0.0, values)
                sums = jnp.sum(values.reshape(TILE // 8, 8, TILE), axis=0)
                total = sums if total is None else total + sums
                probs[rows, lanes] = values.astype(jnp.bfloat16)
            if diagonal:
                acc[:, lanes] = total
            else:
                acc[:, lanes] += total

    y_copies = [
        send(block(0, 0), block(rank, 0), y_send.at[rank], y_recv.at[rank],
             device(0, -ORDER[rank], 0, 0))
        for rank in range(1, NY)
    ]
    pass_on(0)
    z_copies = [
        send(cu.at[pl.ds(0, V)], cu.at[pl.ds(rank * V, V)], z_send.at[rank], z_recv.at[rank],
             device(0, 0, -ORDER[rank], 0))
        for rank in range(1, NZ)
    ]

    def arrived(copies, *ranks):
        for rank in ranks:
            copies[rank - 1].wait_recv()

    for rank in range(1, NY):
        arrived(y_copies, rank)
        pass_on(rank)
    share_when_whole(0)
    share_when_whole(1)
    share(0).wait_recv()
    arrived(z_copies, *range(1, NZ))
    scores(0, True)

    def step(rank, carry):
        @pl.when(rank < NY - 1)
        def _():
            share_when_whole(rank + 1)

        share(rank).wait_recv()
        scores(rank)
        return carry

    lax.fori_loop(1, NY, step, 0)

    sums = jnp.sum(acc[...], axis=0, keepdims=True)
    for rank, part in enumerate(to_rows([sums[:, at:at + W] for at in range(0, ROWS, W)])):
        tps[rank] = part
    p_totals = []
    for rank in range(NZ - 1, -1, -1):
        if rank:
            p_totals.append(send(tps, tp.at[rank], tp_send.at[rank], tp_recv.at[rank],
                                 device(0, 0, ORDER[rank], 0)))
        p_totals.append(send(tps.at[pl.ds(rank, 1)], to.at[pl.ds(rank, 1)], tc_send.at[rank],
                             tc_recv.at[rank], device(0, 0, ORDER[rank], 1)))

    partner_copy.wait()
    pairs = lax.broadcasted_iota(jnp.int32, (V, V), 0) + (row * (NY * 2 * NC) + col) * V
    pairs = (pairs == partner_ref[...]).astype(jnp.bfloat16)
    own_unit = ur[pl.ds(0, V), :]
    partner_unit = jnp.dot(pairs, own_unit, preferred_element_type=jnp.float32)
    positive = lax.dot_general(
        jnp.ones((8, W), jnp.float32), own_unit.astype(jnp.float32) * partner_unit, (((1,), (1,)), ((), ())),
        precision=lax.Precision.HIGHEST, preferred_element_type=jnp.float32,
    )[:1] * inv_temp

    def plain_sums(*lanes):
        for lane in lanes:
            plain[:, pl.ds(lane, TILE)] = jnp.dot(
                ut[...], probs[:, pl.ds(lane, TILE)], preferred_element_type=jnp.float32
            )

    plain_sums(0, TILE)
    for copy in started:
        copy.wait_send()
    for rank in range(NY):
        for dx in (1, 3, 2):
            to_x(rank, dx).wait_send()
        share(rank).wait_send()
    for copy in p_totals:
        copy.wait_recv()
    where = {offset: rank for rank, offset in enumerate(ORDER)}

    def totals_for(rank):
        total = tps[rank]
        for sender in range(1, NZ):
            total = total + tp[sender, where[(ORDER[rank] + ORDER[sender]) % NZ]]
        return total

    totals = totals_for(0)
    tr[0] = jnp.concatenate([totals, jnp.sum(to[...], axis=0)], axis=0)
    for rank in range(NY - 1, -1, -1):
        for dx in (2, 1, 3, 0):
            if rank or dx:
                remote(tr.at[pl.ds(0, 1)], tr.at[pl.ds(rank * NX + dx, 1)], tr_send, tr_recv,
                       device(-dx, -ORDER[rank], 0, 0)).start()
    losses_ref[...] = jnp.log(totals[:, :V]) - positive
    inverse = [1.0 / part for part in to_lanes([totals] + [totals_for(rank) for rank in range(1, NZ)])]
    plain_sums(2 * TILE)

    rest = remote(tr.at[pl.ds(1, NX * NY - 1)], tr.at[pl.ds(1, NX * NY - 1)], tr_send, tr_recv,
                  (row, col))
    rest.wait_recv()
    shares_of = tr[...].reshape(NY, NX, NC, W)
    scales = [1.0 / part for part in to_lanes([shares_of[:, dx] for dx in range(NX)])]
    for at in range(0, COLS, W):
        group, tile = at // GROUP, at % GROUP // W
        factor = scales[tile][group // NC, group % NC:group % NC + 1]
        uts[:, pl.ds(at, W)] = (ut[:, pl.ds(at, W)].astype(jnp.float32) * factor).astype(
            jnp.bfloat16
        )

    outputs = []
    for lane in range(ROWS - TILE, -1, -TILE):
        lanes = pl.ds(lane, TILE)
        sums = jnp.dot(uts[...], probs[:, lanes], preferred_element_type=jnp.float32)
        factor = jnp.concatenate(inverse[lane // W:(lane + TILE) // W], axis=1)
        part = jnp.transpose(plain[:, lanes] * factor + sums)
        sbuf[lanes, :] = part.astype(jnp.bfloat16)
        for rank in range(NZ - 1, 0, -1):
            if lane <= rank * V < lane + TILE:
                at = pl.ds(rank * V, V)
                copy = send(sbuf.at[at], rbuf.at[at], o_send.at[rank], o_recv.at[rank],
                            device(0, 0, ORDER[rank], 0))
                outputs.append((rank, copy))
    kept = part[:V]
    result = kept - 2.0 * partner_unit
    for rank, copy in outputs:
        copy.wait_recv()
        result = result + rbuf[pl.ds(rank * V, V), :].astype(jnp.float32)
    dunit = result * inv_temp
    proj = proj_ref[...]
    scale = lax.rsqrt(jnp.sum(proj * proj, axis=1, keepdims=True) + epsilon)
    inner = jnp.sum(proj * dunit, axis=1, keepdims=True)
    grad_ref[...] = scale * dunit - scale * scale * scale * proj * inner

    for _, copy in outputs:
        copy.wait_send()
    rest.wait_send()


def body(projections, partner):
    dma = pltpu.SemaphoreType.DMA
    projections = pltpu.with_memory_space_constraint(projections, pltpu.HBM)
    partner = pltpu.with_memory_space_constraint(partner.reshape(1, V), pltpu.HBM)
    losses, grad = pl.pallas_call(
        kernel,
        out_shape=(pltpu.VMEM((1, V), jnp.float32), pltpu.VMEM((V, W), jnp.float32)),
        in_specs=[pl.BlockSpec(memory_space=pl.ANY)] * 2,
        out_specs=(pl.BlockSpec(memory_space=pltpu.VMEM),) * 2,
        scratch_shapes=[
            pltpu.VMEM((V, W), jnp.float32),
            pltpu.VMEM((1, V), jnp.int32),
            pltpu.VMEM((COLS, W), jnp.bfloat16),
            pltpu.VMEM((ROWS, W), jnp.bfloat16),
            pltpu.VMEM((COLS, ROWS), jnp.bfloat16),
            pltpu.VMEM((8, ROWS), jnp.float32),
            pltpu.VMEM((W, COLS), jnp.bfloat16),
            pltpu.VMEM((W, COLS), jnp.bfloat16),
            pltpu.VMEM((W, ROWS), jnp.float32),
            pltpu.VMEM((NZ, 1, W), jnp.float32),
            pltpu.VMEM((NZ, NZ, 1, W), jnp.float32),
            pltpu.VMEM((NZ, 1, W), jnp.float32),
            pltpu.VMEM((NY * NX, NC, W), jnp.float32),
            pltpu.VMEM((ROWS, W), jnp.bfloat16),
            pltpu.VMEM((ROWS, W), jnp.bfloat16),
            dma((2,)), dma((NY, NX)), dma((NY, NX)), dma((NY,)), dma((NY,)), dma((NY,)), dma((NY,)),
            dma((NZ,)), dma((NZ,)), dma((NZ,)), dma((NZ,)), dma, dma, dma((NZ,)), dma((NZ,)),
            dma((NZ,)), dma((NZ,)),
        ],
        compiler_params=pltpu.CompilerParams(
            collective_id=0, has_side_effects=True, vmem_limit_bytes=48 * 1024 * 1024
        ),
    )(projections, partner)
    return losses.reshape(V), grad


def solution(mesh):
    in_specs = (P(("row", "col"), None), P(("row", "col")))
    out_specs = (P(("row", "col")), P(("row", "col"), None))
    return jax.shard_map(body, mesh=mesh, in_specs=in_specs, out_specs=out_specs, check_vma=False)
```

```python
import functools

import jax
import jax.numpy as jnp
from jax import lax
from jax.experimental import pallas as pl
from jax.experimental.pallas import tpu as pltpu
from jax.sharding import PartitionSpec as P

inv_temp = 10.0
epsilon = 1e-06
log2e = 1.4426950408889634

V = 96
W = 128
NX, NY, NZ, NC = 4, 8, 8, 2
NR = NX * NY * NC
GROUP = NX * V
BLOCK = NC * GROUP
COLS = NR * V
ROWS = NZ * V
TILE = 256
ORDER = (0, 1, 7, 2, 6, 3, 5, 4)

MESH = pl.DeviceIdType.MESH


def to_rows(tiles):
    rows = []
    for at in range(0, len(tiles), 3):
        first, second, third = tiles[at:at + 3]
        lane = lax.broadcasted_iota(jnp.int32, first.shape, first.ndim - 1)
        turn = functools.partial(pltpu.roll, axis=first.ndim - 1)
        rows.append(first)
        rows.append(jnp.where(lane < 32, turn(first, 32), turn(second, 32)))
        rows.append(jnp.where(lane < 64, turn(second, 64), turn(third, 64)))
        rows.append(turn(third, 96))
    return rows


def to_lanes(rows):
    tiles = []
    for at in range(0, len(rows), 4):
        first, second, third, fourth = rows[at:at + 4]
        lane = lax.broadcasted_iota(jnp.int32, first.shape, first.ndim - 1)
        turn = functools.partial(pltpu.roll, axis=first.ndim - 1)
        second, third, fourth = turn(second, 96), turn(third, 64), turn(fourth, 32)
        tiles.append(jnp.where(lane < 96, first, second))
        tiles.append(jnp.where(lane < 64, second, third))
        tiles.append(jnp.where(lane < 32, third, fourth))
    return tiles


def kernel(
    proj_hbm, partner_hbm, losses_ref, grad_ref,
    proj_ref, partner_ref, ur, cu, probs, acc, both, invr, scale_of, own_part, tps, tp, to, tr, sbuf, rbuf,
    in_sem, x_send, x_recv, y_send, y_recv, k_send, k_recv, z_send, z_recv,
    tp_send, tp_recv, tr_send, tr_recv, tc_send, tc_recv, o_send, o_recv,
):
    proj_copy = pltpu.make_async_copy(proj_hbm, proj_ref, in_sem.at[0])
    partner_copy = pltpu.make_async_copy(partner_hbm, partner_ref, in_sem.at[1])
    proj_copy.start()
    partner_copy.start()

    row, col = lax.axis_index("row"), lax.axis_index("col")
    z, x_lo = row % NZ, row // NZ
    core, x_hi, y = col % NC, (col // NC) % 2, col // (2 * NC)
    x = x_hi * 2 + x_lo
    at_x = [(x + dx) % NX for dx in range(NX)]
    x_row = [(px % 2) * NZ for px in at_x]
    x_col = [(px // 2) * NC for px in at_x]
    y_col = [((y + dy) % NY) * (2 * NC) for dy in range(NY)]
    at_z = [(z + dz) % NZ for dz in range(NZ)]
    cores = (core, 1 - core)

    def device(dx, dy, dz, dk):
        return (x_row[dx % NX] + at_z[dz % NZ], y_col[dy % NY] + x_col[dx % NX] + cores[dk])

    started = []

    def remote(src, dst, send_sem, recv_sem, to):
        return pltpu.make_async_remote_copy(
            src_ref=src, dst_ref=dst, send_sem=send_sem, recv_sem=recv_sem,
            device_id=to, device_id_type=MESH,
        )

    def send(*args):
        copy = remote(*args)
        copy.start()
        started.append(copy)
        return copy

    barrier = pltpu.get_barrier_semaphore()
    peers = [device(dx, 0, 0, 0) for dx in range(1, NX)]
    peers += [device(0, dy, 0, 0) for dy in range(1, NY)]
    peers += [device(0, 0, dz, 0) for dz in range(1, NZ)]
    peers += [device(0, 0, 0, 1)]
    for peer in peers:
        pl.semaphore_signal(barrier, inc=1, device_id=peer, device_id_type=MESH)

    tps[...] = jnp.ones_like(tps)
    acc[...] = jnp.zeros_like(acc)
    proj_copy.wait()
    proj = proj_ref[...]
    scale = lax.rsqrt(jnp.sum(proj * proj, axis=1, keepdims=True) + epsilon)
    unit = (proj * scale).astype(jnp.bfloat16)
    ur[pl.ds(0, V), :] = unit
    cu[pl.ds(0, V), :] = unit

    pl.semaphore_wait(barrier, len(peers))

    def block(rank, dx):
        return ur.at[pl.ds(rank * BLOCK + dx * V, V)]

    def to_x(rank, dx):
        return remote(block(rank, 0), block(rank, dx), x_send.at[rank, dx], x_recv.at[rank, dx],
                      device(-dx, 0, 0, 0))

    def pass_on(rank):
        for dx in (1, 3, 2):
            to_x(rank, dx).start()

    def share(rank):
        first = rank * BLOCK
        return remote(ur.at[pl.ds(first, GROUP)], ur.at[pl.ds(first + GROUP, GROUP)],
                      k_send.at[rank], k_recv.at[rank], device(0, 0, 0, 1))

    def share_when_whole(rank):
        for dx in (1, 3, 2):
            to_x(rank, dx).wait_recv()
        share(rank).start()

    def scores(rank):
        first = pl.multiple_of(rank * BLOCK, BLOCK)
        last = jnp.where(rank == 0, V, 0)
        both[pl.ds(0, W), pl.ds(first, BLOCK)] = jnp.transpose(ur[pl.ds(first, BLOCK), :])
        for lane in range(0, ROWS, TILE):
            lanes = pl.ds(lane, TILE)
            others = cu[lanes, :]
            total = None
            for at in range(0, BLOCK, TILE):
                rows = pl.ds(first + at, TILE)
                dots = lax.dot_general(
                    ur[rows, :], others, (((1,), (1,)), ((), ())),
                    preferred_element_type=jnp.float32,
                )
                values = jnp.exp2(dots * (inv_temp * log2e))
                if lane == 0 and at == 0:
                    left = lax.broadcasted_iota(jnp.int32, (TILE, TILE), 0)
                    right = lax.broadcasted_iota(jnp.int32, (TILE, TILE), 1)
                    values = jnp.where((left == right) & (left < last), 0.0, values)
                sums = jnp.sum(values.reshape(TILE // 8, 8, TILE), axis=0)
                total = sums if total is None else total + sums
                probs[rows, lanes] = values.astype(jnp.bfloat16)
            acc[:, lanes] += total

    y_copies = [
        send(block(0, 0), block(rank, 0), y_send.at[rank], y_recv.at[rank],
             device(0, -ORDER[rank], 0, 0))
        for rank in range(1, NY)
    ]
    pass_on(0)
    z_copies = [
        send(cu.at[pl.ds(0, V)], cu.at[pl.ds(rank * V, V)], z_send.at[rank], z_recv.at[rank],
             device(0, 0, -ORDER[rank], 0))
        for rank in range(1, NZ)
    ]

    def arrived(copies, *ranks):
        for rank in ranks:
            copies[rank - 1].wait_recv()

    for rank in range(1, NY):
        arrived(y_copies, rank)
        pass_on(rank)
    share_when_whole(0)
    arrived(z_copies, *range(1, NZ))

    def step(rank, carry):
        @pl.when(rank < NY - 1)
        def _():
            share_when_whole(rank + 1)

        share(rank).wait_recv()
        scores(rank)
        return carry

    lax.fori_loop(0, NY, step, 0)

    sums = jnp.sum(acc[...], axis=0, keepdims=True)
    for rank, part in enumerate(to_rows([sums[:, at:at + W] for at in range(0, ROWS, W)])):
        tps[rank] = part
    p_totals = []
    for rank in range(NZ - 1, -1, -1):
        if rank:
            p_totals.append(send(tps, tp.at[rank], tp_send.at[rank], tp_recv.at[rank],
                                 device(0, 0, ORDER[rank], 0)))
        p_totals.append(send(tps.at[pl.ds(rank, 1)], to.at[pl.ds(rank, 1)], tc_send.at[rank],
                             tc_recv.at[rank], device(0, 0, ORDER[rank], 1)))

    partner_copy.wait()
    pairs = lax.broadcasted_iota(jnp.int32, (V, V), 0) + (row * (NY * 2 * NC) + col) * V
    pairs = (pairs == partner_ref[...]).astype(jnp.bfloat16)
    own_unit = ur[pl.ds(0, V), :]
    partner_unit = jnp.dot(pairs, own_unit, preferred_element_type=jnp.float32)
    positive = lax.dot_general(
        jnp.ones((8, W), jnp.float32), own_unit.astype(jnp.float32) * partner_unit, (((1,), (1,)), ((), ())),
        precision=lax.Precision.HIGHEST, preferred_element_type=jnp.float32,
    )[:1] * inv_temp

    for copy in started:
        copy.wait_send()
    for rank in range(NY):
        for dx in (1, 3, 2):
            to_x(rank, dx).wait_send()
        share(rank).wait_send()
    for copy in p_totals:
        copy.wait_recv()
    where = {offset: rank for rank, offset in enumerate(ORDER)}

    def totals_for(rank):
        total = tps[rank]
        for sender in range(1, NZ):
            total = total + tp[sender, where[(ORDER[rank] + ORDER[sender]) % NZ]]
        return total

    totals = totals_for(0)
    tr[0] = jnp.concatenate([totals, jnp.sum(to[...], axis=0)], axis=0)
    for rank in range(NY - 1, -1, -1):
        for dx in (2, 1, 3, 0):
            if rank or dx:
                remote(tr.at[pl.ds(0, 1)], tr.at[pl.ds(rank * NX + dx, 1)], tr_send, tr_recv,
                       device(-dx, -ORDER[rank], 0, 0)).start()
    losses_ref[...] = jnp.log(totals[:, :V]) - positive
    inverse = [1.0 / part for part in to_lanes([totals] + [totals_for(rank) for rank in range(1, NZ)])]
    for index, part in enumerate(inverse):
        invr[:, pl.ds(index * W, W)] = part

    rest = remote(tr.at[pl.ds(1, NX * NY - 1)], tr.at[pl.ds(1, NX * NY - 1)], tr_send, tr_recv,
                  (row, col))
    rest.wait_recv()
    shares_of = tr[...].reshape(NY, NX, NC, W)
    scales = [1.0 / part for part in to_lanes([shares_of[:, dx] for dx in range(NX)])]
    for tile, part in enumerate(scales):
        scale_of[tile] = part

    def scaled(rank, carry):
        for k in range(NC):
            for tile in range(GROUP // W):
                at = pl.ds(pl.multiple_of(rank * BLOCK, BLOCK) + k * GROUP + tile * W, W)
                factor = scale_of[tile, rank][k:k + 1]
                both[pl.ds(W, W), at] = (
                    both[pl.ds(0, W), at].astype(jnp.float32) * factor
                ).astype(jnp.bfloat16)
        return carry

    lax.fori_loop(0, NY, scaled, 0)

    outputs = [
        (rank, remote(sbuf.at[pl.ds(rank * V, V)], rbuf.at[pl.ds(rank * V, V)], o_send.at[rank],
                      o_recv.at[rank], device(0, 0, ORDER[rank], 0)))
        for rank in range(NZ - 1, 0, -1)
    ]
    tiles = ROWS // TILE

    def weighted(now, carry):
        lanes = pl.ds(pl.multiple_of((tiles - 1 - now) * TILE, TILE), TILE)
        sums = jnp.dot(both[...], probs[:, lanes], preferred_element_type=jnp.float32)
        part = jnp.transpose(sums[:W] * invr[:, lanes] + sums[W:])
        sbuf[lanes, :] = part.astype(jnp.bfloat16)
        own_part[...] = part
        for tile in range(tiles):
            @pl.when(now == tiles - 1 - tile)
            def _():
                for rank, copy in outputs:
                    if tile * TILE <= rank * V < (tile + 1) * TILE:
                        copy.start()
        return carry

    lax.fori_loop(0, tiles, weighted, 0)
    kept = own_part[pl.ds(0, V), :]
    result = kept - 2.0 * partner_unit
    for rank, copy in outputs:
        copy.wait_recv()
        result = result + rbuf[pl.ds(rank * V, V), :].astype(jnp.float32)
    dunit = result * inv_temp
    proj = proj_ref[...]
    scale = lax.rsqrt(jnp.sum(proj * proj, axis=1, keepdims=True) + epsilon)
    inner = jnp.sum(proj * dunit, axis=1, keepdims=True)
    grad_ref[...] = scale * dunit - scale * scale * scale * proj * inner

    for _, copy in outputs:
        copy.wait_send()
    rest.wait_send()


def body(projections, partner):
    dma = pltpu.SemaphoreType.DMA
    projections = pltpu.with_memory_space_constraint(projections, pltpu.HBM)
    partner = pltpu.with_memory_space_constraint(partner.reshape(1, V), pltpu.HBM)
    losses, grad = pl.pallas_call(
        kernel,
        out_shape=(pltpu.VMEM((1, V), jnp.float32), pltpu.VMEM((V, W), jnp.float32)),
        in_specs=[pl.BlockSpec(memory_space=pl.ANY)] * 2,
        out_specs=(pl.BlockSpec(memory_space=pltpu.VMEM),) * 2,
        scratch_shapes=[
            pltpu.VMEM((V, W), jnp.float32),
            pltpu.VMEM((1, V), jnp.int32),
            pltpu.VMEM((COLS, W), jnp.bfloat16),
            pltpu.VMEM((ROWS, W), jnp.bfloat16),
            pltpu.VMEM((COLS, ROWS), jnp.bfloat16),
            pltpu.VMEM((8, ROWS), jnp.float32),
            pltpu.VMEM((2 * W, COLS), jnp.bfloat16),
            pltpu.VMEM((1, ROWS), jnp.float32),
            pltpu.VMEM((GROUP // W, NY, NC, W), jnp.float32),
            pltpu.VMEM((TILE, W), jnp.float32),
            pltpu.VMEM((NZ, 1, W), jnp.float32),
            pltpu.VMEM((NZ, NZ, 1, W), jnp.float32),
            pltpu.VMEM((NZ, 1, W), jnp.float32),
            pltpu.VMEM((NY * NX, NC, W), jnp.float32),
            pltpu.VMEM((ROWS, W), jnp.bfloat16),
            pltpu.VMEM((ROWS, W), jnp.bfloat16),
            dma((2,)), dma((NY, NX)), dma((NY, NX)), dma((NY,)), dma((NY,)), dma((NY,)), dma((NY,)),
            dma((NZ,)), dma((NZ,)), dma((NZ,)), dma((NZ,)), dma, dma, dma((NZ,)), dma((NZ,)),
            dma((NZ,)), dma((NZ,)),
        ],
        compiler_params=pltpu.CompilerParams(
            collective_id=0, has_side_effects=True, vmem_limit_bytes=48 * 1024 * 1024
        ),
    )(projections, partner)
    return losses.reshape(V), grad


def solution(mesh):
    in_specs = (P(("row", "col"), None), P(("row", "col")))
    out_specs = (P(("row", "col")), P(("row", "col"), None))
    return jax.shard_map(body, mesh=mesh, in_specs=in_specs, out_specs=out_specs, check_vma=False)
```

```python
import functools

import jax
import jax.numpy as jnp
from jax import lax
from jax.experimental import pallas as pl
from jax.experimental.pallas import tpu as pltpu
from jax.sharding import PartitionSpec as P

inv_temp = 10.0
epsilon = 1e-06
log2e = 1.4426950408889634

V = 96
W = 128
NX, NY, NZ, NC = 4, 8, 8, 2
NR = NX * NY * NC
GROUP = NX * V
BLOCK = NC * GROUP
COLS = NR * V
ROWS = NZ * V
TILE = 256
ORDER = (0, 1, 7, 2, 6, 3, 5, 4)

MESH = pl.DeviceIdType.MESH


def to_rows(tiles):
    rows = []
    for at in range(0, len(tiles), 3):
        first, second, third = tiles[at:at + 3]
        lane = lax.broadcasted_iota(jnp.int32, first.shape, first.ndim - 1)
        turn = functools.partial(pltpu.roll, axis=first.ndim - 1)
        rows.append(first)
        rows.append(jnp.where(lane < 32, turn(first, 32), turn(second, 32)))
        rows.append(jnp.where(lane < 64, turn(second, 64), turn(third, 64)))
        rows.append(turn(third, 96))
    return rows


def to_lanes(rows):
    tiles = []
    for at in range(0, len(rows), 4):
        first, second, third, fourth = rows[at:at + 4]
        lane = lax.broadcasted_iota(jnp.int32, first.shape, first.ndim - 1)
        turn = functools.partial(pltpu.roll, axis=first.ndim - 1)
        second, third, fourth = turn(second, 96), turn(third, 64), turn(fourth, 32)
        tiles.append(jnp.where(lane < 96, first, second))
        tiles.append(jnp.where(lane < 64, second, third))
        tiles.append(jnp.where(lane < 32, third, fourth))
    return tiles


def kernel(
    proj_hbm, partner_hbm, losses_ref, grad_ref,
    proj_ref, partner_ref, ur, cu, cut, probs, acc, ut, uts, plain, tps, tp, to, tr, sbuf, rbuf,
    in_sem, x_send, x_recv, y_send, y_recv, k_send, k_recv, z_send, z_recv,
    tp_send, tp_recv, tr_send, tr_recv, tc_send, tc_recv, o_send, o_recv,
):
    proj_copy = pltpu.make_async_copy(proj_hbm, proj_ref, in_sem.at[0])
    partner_copy = pltpu.make_async_copy(partner_hbm, partner_ref, in_sem.at[1])
    proj_copy.start()
    partner_copy.start()

    row, col = lax.axis_index("row"), lax.axis_index("col")
    z, x_lo = row % NZ, row // NZ
    core, x_hi, y = col % NC, (col // NC) % 2, col // (2 * NC)
    x = x_hi * 2 + x_lo
    at_x = [(x + dx) % NX for dx in range(NX)]
    x_row = [(px % 2) * NZ for px in at_x]
    x_col = [(px // 2) * NC for px in at_x]
    y_col = [((y + dy) % NY) * (2 * NC) for dy in range(NY)]
    at_z = [(z + dz) % NZ for dz in range(NZ)]
    cores = (core, 1 - core)

    def device(dx, dy, dz, dk):
        return (x_row[dx % NX] + at_z[dz % NZ], y_col[dy % NY] + x_col[dx % NX] + cores[dk])

    started = []

    def remote(src, dst, send_sem, recv_sem, to):
        return pltpu.make_async_remote_copy(
            src_ref=src, dst_ref=dst, send_sem=send_sem, recv_sem=recv_sem,
            device_id=to, device_id_type=MESH,
        )

    def send(*args):
        copy = remote(*args)
        copy.start()
        started.append(copy)
        return copy

    barrier = pltpu.get_barrier_semaphore()
    peers = [device(dx, 0, 0, 0) for dx in range(1, NX)]
    peers += [device(0, dy, 0, 0) for dy in range(1, NY)]
    peers += [device(0, 0, dz, 0) for dz in range(1, NZ)]
    peers += [device(0, 0, 0, 1)]
    for peer in peers:
        pl.semaphore_signal(barrier, inc=1, device_id=peer, device_id_type=MESH)

    tps[...] = jnp.ones_like(tps)
    proj_copy.wait()
    proj = proj_ref[...]
    scale = lax.rsqrt(jnp.sum(proj * proj, axis=1, keepdims=True) + epsilon)
    unit = (proj * scale).astype(jnp.bfloat16)
    ur[pl.ds(0, V), :] = unit
    cu[pl.ds(0, V), :] = unit

    pl.semaphore_wait(barrier, len(peers))

    def block(rank, dx):
        return ur.at[pl.ds(rank * BLOCK + dx * V, V)]

    def to_x(rank, dx):
        return remote(block(rank, 0), block(rank, dx), x_send.at[rank, dx], x_recv.at[rank, dx],
                      device(-dx, 0, 0, 0))

    def pass_on(rank):
        for dx in (1, 3, 2):
            to_x(rank, dx).start()

    def share(rank):
        first = rank * BLOCK
        return remote(ur.at[pl.ds(first, GROUP)], ur.at[pl.ds(first + GROUP, GROUP)],
                      k_send.at[rank], k_recv.at[rank], device(0, 0, 0, 1))

    def share_when_whole(rank):
        for dx in (1, 3, 2):
            to_x(rank, dx).wait_recv()
        share(rank).start()

    def turned(lane):
        cut[:, pl.ds(lane, TILE)] = jnp.transpose(cu[pl.ds(lane, TILE), :])

    def scores(rank, k, tiles=range(0, ROWS, TILE)):
        first_group = isinstance(rank, int) and rank == 0 and k == 0
        first = pl.multiple_of((rank * NC + k) * GROUP, GROUP)
        rows = pl.ds(first, GROUP)
        units = ur[rows, :]
        if 0 in tiles:
            ut[:, rows] = jnp.transpose(units)
        for lane in tiles:
            lanes = pl.ds(lane, TILE)
            dots = jnp.dot(units, cut[:, lanes], preferred_element_type=jnp.float32)
            values = jnp.exp2(dots * (inv_temp * log2e))
            if first_group and lane == 0:
                left = lax.broadcasted_iota(jnp.int32, (GROUP, TILE), 0)
                right = lax.broadcasted_iota(jnp.int32, (GROUP, TILE), 1)
                values = jnp.where((left == right) & (left < V), 0.0, values)
            total = jnp.sum(values.reshape(GROUP // 8, 8, TILE), axis=0)
            probs[rows, lanes] = values.astype(jnp.bfloat16)
            if first_group:
                acc[:, lanes] = total
            else:
                acc[:, lanes] += total

    y_copies = [
        send(block(0, 0), block(rank, 0), y_send.at[rank], y_recv.at[rank],
             device(0, -ORDER[rank], 0, 0))
        for rank in range(1, NY)
    ]
    pass_on(0)
    z_copies = [
        send(cu.at[pl.ds(0, V)], cu.at[pl.ds(rank * V, V)], z_send.at[rank], z_recv.at[rank],
             device(0, 0, -ORDER[rank], 0))
        for rank in range(1, NZ)
    ]

    def arrived(copies, *ranks):
        for rank in ranks:
            copies[rank - 1].wait_recv()

    def go_on(*ranks):
        for rank in ranks:
            arrived(y_copies, rank)
            pass_on(rank)

    go_on(1, 2)
    share_when_whole(0)
    arrived(z_copies, 1, 2)
    turned(0)
    scores(0, 0, (0,))
    go_on(3, 4)
    arrived(z_copies, 3, 4, 5)
    turned(TILE)
    scores(0, 0, (TILE,))
    go_on(5, 6)
    share(0).wait_recv()
    scores(0, 1, (0, TILE))
    go_on(7)
    arrived(z_copies, 6, 7)
    turned(2 * TILE)
    scores(0, 0, (2 * TILE,))
    scores(0, 1, (2 * TILE,))

    def own_core(rank, carry):
        share_when_whole(rank)
        scores(rank, 0)
        return carry

    def other_core(rank, carry):
        share(rank).wait_recv()
        scores(rank, 1)
        return carry

    def both_cores(rank, carry):
        own_core(rank, carry)
        other_core(rank - 1, carry)
        return carry

    own_core(1, 0)
    lax.fori_loop(2, NY, both_cores, 0)
    other_core(NY - 1, 0)

    sums = jnp.sum(acc[...], axis=0, keepdims=True)
    for rank, part in enumerate(to_rows([sums[:, at:at + W] for at in range(0, ROWS, W)])):
        tps[rank] = part
    p_totals = []
    for rank in range(NZ - 1, -1, -1):
        if rank:
            p_totals.append(send(tps, tp.at[rank], tp_send.at[rank], tp_recv.at[rank],
                                 device(0, 0, ORDER[rank], 0)))
        p_totals.append(send(tps.at[pl.ds(rank, 1)], to.at[pl.ds(rank, 1)], tc_send.at[rank],
                             tc_recv.at[rank], device(0, 0, ORDER[rank], 1)))

    partner_copy.wait()
    pairs = lax.broadcasted_iota(jnp.int32, (V, V), 0) + (row * (NY * 2 * NC) + col) * V
    pairs = (pairs == partner_ref[...]).astype(jnp.bfloat16)
    own_unit = ur[pl.ds(0, V), :]
    partner_unit = jnp.dot(pairs, own_unit, preferred_element_type=jnp.float32)
    positive = lax.dot_general(
        jnp.ones((8, W), jnp.float32), own_unit.astype(jnp.float32) * partner_unit, (((1,), (1,)), ((), ())),
        precision=lax.Precision.HIGHEST, preferred_element_type=jnp.float32,
    )[:1] * inv_temp

    def plain_sums(*lanes):
        for lane in lanes:
            plain[:, pl.ds(lane, TILE)] = jnp.dot(
                ut[...], probs[:, pl.ds(lane, TILE)], preferred_element_type=jnp.float32
            )

    plain_sums(0, TILE)
    for copy in started:
        copy.wait_send()
    for rank in range(NY):
        for dx in (1, 3, 2):
            to_x(rank, dx).wait_send()
        share(rank).wait_send()
    for copy in p_totals:
        copy.wait_recv()
    where = {offset: rank for rank, offset in enumerate(ORDER)}

    def totals_for(rank):
        total = tps[rank]
        for sender in range(1, NZ):
            total = total + tp[sender, where[(ORDER[rank] + ORDER[sender]) % NZ]]
        return total

    totals = totals_for(0)
    tr[0] = jnp.concatenate([totals, jnp.sum(to[...], axis=0)], axis=0)
    for rank in range(NY - 1, -1, -1):
        for dx in (2, 1, 3, 0):
            if rank or dx:
                remote(tr.at[pl.ds(0, 1)], tr.at[pl.ds(rank * NX + dx, 1)], tr_send, tr_recv,
                       device(-dx, -ORDER[rank], 0, 0)).start()
    losses_ref[...] = jnp.log(totals[:, :V]) - positive
    inverse = [1.0 / part for part in to_lanes([totals] + [totals_for(rank) for rank in range(1, NZ)])]
    plain_sums(2 * TILE)

    rest = remote(tr.at[pl.ds(1, NX * NY - 1)], tr.at[pl.ds(1, NX * NY - 1)], tr_send, tr_recv,
                  (row, col))
    rest.wait_recv()
    shares_of = tr[...].reshape(NY, NX, NC, W)
    scales = [1.0 / part for part in to_lanes([shares_of[:, dx] for dx in range(NX)])]
    for at in range(0, COLS, W):
        group, tile = at // GROUP, at % GROUP // W
        factor = scales[tile][group // NC, group % NC:group % NC + 1]
        uts[:, pl.ds(at, W)] = (ut[:, pl.ds(at, W)].astype(jnp.float32) * factor).astype(
            jnp.bfloat16
        )

    outputs = []
    for lane in range(ROWS - TILE, -1, -TILE):
        lanes = pl.ds(lane, TILE)
        sums = jnp.dot(uts[...], probs[:, lanes], preferred_element_type=jnp.float32)
        factor = jnp.concatenate(inverse[lane // W:(lane + TILE) // W], axis=1)
        part = jnp.transpose(plain[:, lanes] * factor + sums)
        sbuf[lanes, :] = part.astype(jnp.bfloat16)
        for rank in range(NZ - 1, 0, -1):
            if lane <= rank * V < lane + TILE:
                at = pl.ds(rank * V, V)
                copy = send(sbuf.at[at], rbuf.at[at], o_send.at[rank], o_recv.at[rank],
                            device(0, 0, ORDER[rank], 0))
                outputs.append((rank, copy))
    kept = part[:V]
    result = kept - 2.0 * partner_unit
    for rank, copy in outputs:
        copy.wait_recv()
        result = result + rbuf[pl.ds(rank * V, V), :].astype(jnp.float32)
    dunit = result * inv_temp
    proj = proj_ref[...]
    scale = lax.rsqrt(jnp.sum(proj * proj, axis=1, keepdims=True) + epsilon)
    inner = jnp.sum(proj * dunit, axis=1, keepdims=True)
    grad_ref[...] = scale * dunit - scale * scale * scale * proj * inner

    for _, copy in outputs:
        copy.wait_send()
    rest.wait_send()


def body(projections, partner):
    dma = pltpu.SemaphoreType.DMA
    projections = pltpu.with_memory_space_constraint(projections, pltpu.HBM)
    partner = pltpu.with_memory_space_constraint(partner.reshape(1, V), pltpu.HBM)
    losses, grad = pl.pallas_call(
        kernel,
        out_shape=(pltpu.VMEM((1, V), jnp.float32), pltpu.VMEM((V, W), jnp.float32)),
        in_specs=[pl.BlockSpec(memory_space=pl.ANY)] * 2,
        out_specs=(pl.BlockSpec(memory_space=pltpu.VMEM),) * 2,
        scratch_shapes=[
            pltpu.VMEM((V, W), jnp.float32),
            pltpu.VMEM((1, V), jnp.int32),
            pltpu.VMEM((COLS, W), jnp.bfloat16),
            pltpu.VMEM((ROWS, W), jnp.bfloat16),
            pltpu.VMEM((W, ROWS), jnp.bfloat16),
            pltpu.VMEM((COLS, ROWS), jnp.bfloat16),
            pltpu.VMEM((8, ROWS), jnp.float32),
            pltpu.VMEM((W, COLS), jnp.bfloat16),
            pltpu.VMEM((W, COLS), jnp.bfloat16),
            pltpu.VMEM((W, ROWS), jnp.float32),
            pltpu.VMEM((NZ, 1, W), jnp.float32),
            pltpu.VMEM((NZ, NZ, 1, W), jnp.float32),
            pltpu.VMEM((NZ, 1, W), jnp.float32),
            pltpu.VMEM((NY * NX, NC, W), jnp.float32),
            pltpu.VMEM((ROWS, W), jnp.bfloat16),
            pltpu.VMEM((ROWS, W), jnp.bfloat16),
            dma((2,)), dma((NY, NX)), dma((NY, NX)), dma((NY,)), dma((NY,)), dma((NY,)), dma((NY,)),
            dma((NZ,)), dma((NZ,)), dma((NZ,)), dma((NZ,)), dma, dma, dma((NZ,)), dma((NZ,)),
            dma((NZ,)), dma((NZ,)),
        ],
        compiler_params=pltpu.CompilerParams(
            collective_id=0, has_side_effects=True, vmem_limit_bytes=48 * 1024 * 1024
        ),
    )(projections, partner)
    return losses.reshape(V), grad


def solution(mesh):
    in_specs = (P(("row", "col"), None), P(("row", "col")))
    out_specs = (P(("row", "col")), P(("row", "col"), None))
    return jax.shard_map(body, mesh=mesh, in_specs=in_specs, out_specs=out_specs, check_vma=False)
```
